32 devices in a mesh: gz: 4 (over y, x), gy: 4 (over z), gx: 2 (over core).
Axes of the slice: x: 2, y: 2, z: 4, core: 2. Of those that a mesh axis runs over, the one named last changes fastest.
Arguments:
- section: bfloat16 [4, 1024, 512], P('gz', 'gy', 'gx'), may hold values from -6 to 6
- first_kernel: float32 [16, 9], replicated, may hold values from -2 to 2
- first_bias: float32 [16], replicated, may hold values from -3 to 3
- second_kernel: bfloat16 [9, 16, 16], replicated, may hold values from -0.5 to 0.5
- second_bias: float32 [16], replicated, may hold values from -3 to 3
- head_weight: float32 [16], replicated, may hold values from -1.5 to 1.5
Outputs:
- spectra: float32 [4, 2, 1024, 512], P('gz', None, 'gy', 'gx')
The draws below stay inside these ranges and needn't reach their ends.
All inputs are finite; a program needn't handle non-finite values.
Results may differ from the reference program's by a relative error of at most 0.0075.
Values may be sent and summed in bfloat16 or wider, within the bound.
A program may use at most 128 MiB of HBM per device.

```python
import math
import jax
import jax.numpy as jnp
from jax import lax

CHANNELS = 16
PATCH = 128
ROWS_DEV = 256
COLS_DEV = 256
SECTIONS = 4
HEIGHT = 1024
WIDTH = 512
N_GY = 4
N_GX = 2


def block_scale(key, extent, cuts, low, largest):
    def one(position, blocks):
        draws = jax.random.uniform(jax.random.fold_in(jax.random.fold_in(key, 6), position), (blocks,), jnp.float32, low / len(cuts), largest / len(cuts))
        return jnp.repeat(jnp.exp(draws), extent[position] // blocks).reshape((-1,) + (1,) * (len(extent) - position - 1))

    level = one(*cuts[0])
    for cut in cuts[1:]:
        level = level * one(*cut)
    return level


def scatter_about(own_key, extent, scale, limit, split=(), kind=jnp.bfloat16):
    array = jax.random.normal(own_key, extent, jnp.float32) * scale
    if len(split) > 0:
        array = block_scale(own_key, extent, split, -0.22, 0.18) * array
    return jnp.clip(array, min=-limit, max=limit).astype(kind)


def setup_inputs(seed: int = 0) -> dict:
    streams_of = jax.random.split(jax.random.key(seed), 7)
    section = scatter_about(streams_of[0], (SECTIONS, HEIGHT, WIDTH), 1.0, 6.0, ((0, 4), (1, 4), (2, 2)))
    first_kernel = scatter_about(streams_of[1], (CHANNELS, 9), 9 ** -0.5, 2.0, (), jnp.float32)
    first_bias = scatter_about(streams_of[2], (CHANNELS,), 0.5, 3.0, (), jnp.float32)
    second_kernel = scatter_about(streams_of[3], (9, CHANNELS, CHANNELS), (9 * CHANNELS) ** -0.5, 0.5)
    second_bias = scatter_about(streams_of[4], (CHANNELS,), 0.5, 3.0, (), jnp.float32)
    head_weight = scatter_about(streams_of[5], (CHANNELS,), CHANNELS ** -0.5, 1.5, (), jnp.float32)
    return {"section": section, "first_kernel": first_kernel, "first_bias": first_bias, "second_kernel": second_kernel, "second_bias": second_bias, "head_weight": head_weight}


def dft_tables(length):
    positions = jnp.arange(length, dtype=jnp.int32)
    phase_step = positions[:, None] * positions[None, :] % length
    angles = phase_step.astype(jnp.float32) * (2.0 * math.pi / length)
    scaling = 1.0 / math.sqrt(length)
    cosine_table = (jnp.cos(angles) * scaling).astype(jnp.bfloat16)
    sine_table = (jnp.sin(angles) * scaling).astype(jnp.bfloat16)
    return (cosine_table, sine_table)

def first_layer(padded, kernel, offsets):
    row_count = padded.shape[0] - 2
    col_count = padded.shape[1] - 2
    values = padded.astype(jnp.float32)
    summed = jnp.zeros((kernel.shape[0], row_count, col_count), jnp.float32)
    for tap_index in range(9):
        row_off = tap_index // 3
        col_off = tap_index % 3
        window = values[row_off:row_off + row_count, col_off:col_off + col_count]
        summed = summed + kernel[:, tap_index][:, None, None] * window[None]
    return jax.nn.relu(summed + offsets[:, None, None]).astype(jnp.bfloat16)

def second_layer(hidden_pad, center, kernel, offsets, head_vec):
    row_count = hidden_pad.shape[1] - 2
    col_count = hidden_pad.shape[2] - 2
    summed = jnp.zeros((kernel.shape[1], row_count, col_count), jnp.float32)
    for tap_index in range(9):
        row_off = tap_index // 3
        col_off = tap_index % 3
        window = hidden_pad[:, row_off:row_off + row_count, col_off:col_off + col_count]
        summed = summed + jnp.einsum('oc,crw->orw', kernel[tap_index].astype(jnp.float32), window.astype(jnp.float32))
    deep = jax.nn.relu(summed + offsets[:, None, None])
    return (center.astype(jnp.float32) + lax.optimization_barrier(jnp.sum(head_vec[:, None, None] * deep, axis=0))).astype(jnp.bfloat16)

def restore_block(padded, first_kernel, first_bias, second_kernel, second_bias, head_weight, row_start, col_start, height, full_width):
    hidden = first_layer(padded, first_kernel, first_bias)
    row_ids = row_start - 1 + jnp.arange(hidden.shape[1], dtype=jnp.int32)
    col_ids = col_start - 1 + jnp.arange(hidden.shape[2], dtype=jnp.int32)
    inside = ((row_ids >= 0) & (row_ids < height))[:, None] & ((col_ids >= 0) & (col_ids < full_width))[None, :]
    hidden = jnp.where(inside[None], hidden, jnp.zeros_like(hidden))
    center = padded[2:-2, 2:-2]
    return second_layer(hidden, center, second_kernel, second_bias, head_weight)

def spectrum(restored, cosine_table, sine_table):
    length = cosine_table.shape[0]
    row_count, col_count = restored.shape
    tiles = restored.reshape(row_count // length, length, col_count // length, length).astype(jnp.float32)
    cos_f = cosine_table.astype(jnp.float32)
    sin_f = sine_table.astype(jnp.float32)
    rows_cos = jnp.einsum('aibj,jk->aibk', tiles, cos_f).astype(jnp.bfloat16).astype(jnp.float32)
    rows_sin = jnp.einsum('aibj,jk->aibk', tiles, sin_f).astype(jnp.bfloat16).astype(jnp.float32)
    real_part = jnp.einsum('ij,aibk->ajbk', cos_f, rows_cos) - jnp.einsum('ij,aibk->ajbk', sin_f, rows_sin)
    imag_part = -(jnp.einsum('ij,aibk->ajbk', cos_f, rows_sin) + jnp.einsum('ij,aibk->ajbk', sin_f, rows_cos))
    return jnp.stack([real_part.reshape(row_count, col_count), imag_part.reshape(row_count, col_count)])

def cross(first_spec, second_spec):
    real_out = first_spec[0] * second_spec[0] + first_spec[1] * second_spec[1]
    imag_out = first_spec[1] * second_spec[0] - first_spec[0] * second_spec[1]
    return jnp.stack([real_out, imag_out])

def reference(section, first_kernel, first_bias, second_kernel, second_bias, head_weight):
    height = ROWS_DEV * N_GY
    full_width = COLS_DEV * N_GX
    block_count = height // ROWS_DEV
    cosine_table, sine_table = dft_tables(PATCH)

    def restore_section(section_image):
        padded = jnp.pad(section_image, 2)

        def one_block(block_index):
            row_start = (block_index * ROWS_DEV).astype(jnp.int32)
            rows_pad = lax.dynamic_slice_in_dim(padded, row_start, ROWS_DEV + 4, 0)
            return restore_block(rows_pad, first_kernel, first_bias, second_kernel, second_bias, head_weight, row_start, jnp.int32(0), height, full_width)
        pieces = lax.map(one_block, jnp.arange(block_count, dtype=jnp.int32))
        return pieces.reshape(height, full_width)
    spectra_list = []
    for sec_index in range(SECTIONS):
        spectra_list.append(spectrum(restore_section(section[sec_index]), cosine_table, sine_table))
    outputs = []
    for sec_index in range(SECTIONS):
        if sec_index + 1 < SECTIONS:
            outputs.append(cross(spectra_list[sec_index], spectra_list[sec_index + 1]))
        else:
            outputs.append(jnp.zeros((2, height, full_width), jnp.float32))
    return jnp.stack(outputs)
```

```python
import functools
import math

import jax
import jax.numpy as jnp
import numpy as np
from jax import lax
from jax.experimental import pallas as pl
from jax.experimental.pallas import tpu as pltpu
from jax.sharding import PartitionSpec as P

PATCH = 128
CH = 16
EDGE = 16
LANES = 128
ROWS_OUT = 8
F32 = jnp.float32
BF16 = jnp.bfloat16
MESH = pl.DeviceIdType.MESH
STEPS = [(-1, 0), (1, 0), (0, -1), (0, 1), (-1, -1), (-1, 1), (1, -1), (1, 1)]


def dft_table():
    positions = np.arange(PATCH)
    phase = (positions[:, None] * positions[None, :]) % PATCH
    angles = phase * (2.0 * math.pi / PATCH)
    both = np.concatenate([np.cos(angles), np.sin(angles)], axis=1) / math.sqrt(PATCH)
    return both.astype(np.float32).astype(jnp.bfloat16)


def iota(shape, dim):
    return lax.broadcasted_iota(jnp.int32, shape, dim)


def dot(a, b):
    return jnp.dot(a, b, preferred_element_type=F32)


def pieces(value, count):
    out = []
    for _ in range(count):
        part = value.astype(BF16)
        out.append(part)
        value = value - part.astype(F32)
    return out


def column_of(ref, ids):
    column = jnp.zeros(ids.shape, F32)
    for c in range(CH):
        column = jnp.where(ids == c, ref[c], column)
    return column


def first_weights(kernel_ref, bias_ref):
    rows, depth = 16 * CH, 256
    high, low = pieces(kernel_ref[...], 2)
    k = iota((9, depth), 1)
    tap = iota((9, depth), 0)
    split, col_off = k // 96, (k % 96) // 32
    m = iota((rows, depth), 0)
    kk = iota((rows, depth), 1)
    spread = jnp.where(iota((rows, CH), 0) % CH == iota((rows, CH), 1), 1.0, 0.0).astype(BF16)
    offset = (kk % 96) % 32 - 14 - m // CH
    weights = jnp.zeros((rows, depth), F32)
    for a in range(3):
        hit = tap == 3 * a + col_off
        placed = dot(high, jnp.where(hit & (split == 0), 1.0, 0.0).astype(BF16))
        placed = placed + dot(low, jnp.where(hit & (split == 1), 1.0, 0.0).astype(BF16))
        weights = jnp.where(offset == a, dot(spread, placed.astype(BF16)), weights)
    parts = pieces(column_of(bias_ref, m % CH), 3)
    weights = jnp.where(kk >= 192, 0.0, weights)
    for n, part in enumerate(parts):
        weights = jnp.where(kk == 192 + n, part.astype(F32), weights)
    return weights.astype(BF16)


def second_weights(kernel_ref, bias_ref):
    rows, depth = ROWS_OUT * CH, 512
    flat = kernel_ref[...].reshape(9 * CH, CH)
    tile = jnp.where(iota((CH, depth), 1) % CH == iota((CH, depth), 0), 1.0, 0.0).astype(BF16)
    tiled = dot(flat, tile).astype(BF16)
    spread = jnp.where(iota((rows, CH), 0) // ROWS_OUT == iota((rows, CH), 1), 1.0, 0.0).astype(BF16)
    m = iota((rows, depth), 0)
    kk = iota((rows, depth), 1)
    slot = kk // CH - 3 * (m % ROWS_OUT)
    weights = jnp.zeros((rows, depth), F32)
    for t in range(9):
        weights = jnp.where(slot == t, dot(spread, tiled[t * CH : (t + 1) * CH]), weights)
    parts = pieces(column_of(bias_ref, m // ROWS_OUT), 3)
    weights = jnp.where(kk >= 480, 0.0, weights)
    for n, part in enumerate(parts):
        weights = jnp.where(kk == 480 + n, part.astype(F32), weights)
    return weights.astype(BF16)


def spectrum(image, table):
    cosine, sine = table[:, :PATCH], table[:, PATCH:]
    patches = image.shape[1] // PATCH
    stacked = jnp.concatenate([image[:, n * PATCH : (n + 1) * PATCH] for n in range(patches)], axis=0)
    rows = dot(stacked, table).astype(BF16)
    parts = [rows[n * PATCH : (n + 1) * PATCH] for n in range(patches)]
    lower = jnp.concatenate(
        [
            jnp.concatenate([p[:, :PATCH] for p in parts], axis=1),
            jnp.concatenate([p[:, PATCH:] for p in parts], axis=1),
        ],
        axis=0,
    )
    full = jnp.concatenate(
        [jnp.concatenate([cosine, -sine], axis=1), jnp.concatenate([-sine, -cosine], axis=1)], axis=0
    )
    both = dot(full, lower)
    return both[:PATCH], both[PATCH:]


def body(
    sizes,
    x_ref, k1_ref, k2_ref, table_ref, b1_ref, b2_ref, hw_ref,
    out_ref,
    halo, shifted, hidden, own, following, w1_ref, w2_ref,
    halo_send, halo_recv, next_send, next_recv,
):
    n_gz, n_gy, n_gx = sizes
    height, width = x_ref.shape
    wide = width + LANES
    gz, gy, gx = lax.axis_index("gz"), lax.axis_index("gy"), lax.axis_index("gx")

    def present(dy, dx):
        y, x = gy + dy, gx + dx
        return (y >= 0) & (y < n_gy) & (x >= 0) & (x < n_gx)

    def device(dz, dy, dx):
        return (
            lax.rem(gz + dz + n_gz, n_gz),
            lax.rem(gy + dy + n_gy, n_gy),
            lax.rem(gx + dx + n_gx, n_gx),
        )

    not_first, not_last = gz > 0, gz < n_gz - 1

    barrier = pltpu.get_barrier_semaphore()
    count = not_first.astype(jnp.int32) + not_last.astype(jnp.int32)
    for dy, dx in STEPS:
        count = count + present(dy, dx).astype(jnp.int32)

        @pl.when(present(dy, dx))
        def _():
            pl.semaphore_signal(barrier, inc=1, device_id=device(0, dy, dx), device_id_type=MESH)

    @pl.when(not_first)
    def _():
        pl.semaphore_signal(barrier, inc=1, device_id=device(-1, 0, 0), device_id_type=MESH)

    @pl.when(not_last)
    def _():
        pl.semaphore_signal(barrier, inc=1, device_id=device(1, 0, 0), device_id_type=MESH)

    pl.semaphore_wait(barrier, count)

    row_src = {-1: (0, EDGE), 1: (height - EDGE, EDGE), 0: (0, height)}
    col_src = {-1: (0, LANES), 1: (width - LANES, LANES), 0: (0, width)}
    row_dst = {-1: EDGE + height, 1: 0, 0: EDGE}
    col_dst = {-1: width, 1: width + LANES, 0: 0}
    copies = []
    for n, (dy, dx) in enumerate(STEPS):
        (r0, rn), (c0, cn) = row_src[dy], col_src[dx]
        copies.append(
            pltpu.make_async_remote_copy(
                src_ref=x_ref.at[pl.ds(r0, rn), pl.ds(c0, cn)],
                dst_ref=halo.at[pl.ds(row_dst[dy], rn), pl.ds(col_dst[dx], cn)],
                send_sem=halo_send.at[n],
                recv_sem=halo_recv.at[n],
                device_id=device(0, dy, dx),
                device_id_type=MESH,
            )
        )
    for n, (dy, dx) in enumerate(STEPS):

        @pl.when(present(dy, dx))
        def _():
            copies[n].start()

        @pl.when(jnp.logical_not(present(-dy, -dx)))
        def _():
            rn, cn = row_src[dy][1], col_src[dx][1]
            halo[pl.ds(row_dst[dy], rn), pl.ds(col_dst[dx], cn)] = jnp.zeros((rn, cn), BF16)

    w1_ref[...] = first_weights(k1_ref, b1_ref)
    w2_ref[...] = second_weights(k2_ref, b2_ref)

    for n, (dy, dx) in enumerate(STEPS):

        @pl.when(present(-dy, -dx))
        def _():
            copies[n].wait_recv()

    def place(row, size, centre):
        right = halo[pl.ds(row, size), pl.ds(width, LANES)].astype(F32)
        left = halo[pl.ds(row, size), pl.ds(width + LANES, LANES)].astype(F32)
        side = jnp.where(iota((size, LANES), 1) < LANES // 2, right, left)
        ring = jnp.concatenate([centre.astype(F32), side], axis=1)
        shifted[0, pl.ds(row, size), :] = pltpu.roll(ring, 1, 1).astype(BF16)
        shifted[1, pl.ds(row, size), :] = ring.astype(BF16)
        shifted[2, pl.ds(row, size), :] = pltpu.roll(ring, wide - 1, 1).astype(BF16)

    place(0, EDGE, halo[0:EDGE, 0:width])
    place(EDGE + height, EDGE, halo[EDGE + height : 2 * EDGE + height, 0:width])

    def fill(i, carry):
        place(EDGE + i * 64, 64, x_ref[pl.ds(pl.multiple_of(i * 64, 64), 64), :])
        return carry

    lax.fori_loop(0, height // 64, fill, 0)

    lane = iota((1, wide), 1)
    keep = (lane < width) | ((lane == width) & (gx < n_gx - 1)) | ((lane == wide - 1) & (gx > 0))
    keep = jnp.where(keep, 1.0, 0.0)

    def layer_one(i, rows):
        start = pl.multiple_of(i * 16, 16)
        taps = [shifted[b, pl.ds(start, 32), :] for b in range(3)]
        stack = jnp.concatenate(taps + taps + [jnp.ones((16, wide), BF16)], axis=0)
        value = dot(w1_ref[0 : rows * CH, 0:208], stack)
        value = jnp.maximum(value, 0.0) * keep
        hidden[pl.ds(start, rows), CH : 2 * CH, :] = (
            value[:, :width].astype(BF16).reshape(rows, CH, width)
        )
        hidden[pl.ds(start, rows), 0:CH, :] = (
            pltpu.roll(value, 1, 1)[:, :width].astype(BF16).reshape(rows, CH, width)
        )
        hidden[pl.ds(start, rows), 2 * CH : 3 * CH, :] = (
            pltpu.roll(value, wide - 1, 1)[:, :width].astype(BF16).reshape(rows, CH, width)
        )

    def layer_two(i):
        start = pl.multiple_of(i * 16, 16)
        rows = []
        for g in range(2):
            window = hidden[pl.ds(start + g * ROWS_OUT, ROWS_OUT + 2), :, :].reshape(480, width)
            stack = jnp.concatenate([window, jnp.ones((16, width), BF16)], axis=0)
            deep = jnp.maximum(dot(w2_ref[:, 0:496], stack), 0.0)
            total = hw_ref[0] * deep[0:ROWS_OUT]
            for o in range(1, CH):
                total = total + hw_ref[o] * deep[o * ROWS_OUT : (o + 1) * ROWS_OUT]
            rows.append(total)
        total = jnp.concatenate(rows, axis=0)
        centre = x_ref[pl.ds(start, 16), :].astype(F32)
        own[pl.ds(start, 16), :] = (centre + total).astype(BF16)

    def one(i, carry):
        layer_one(i, 16)
        return carry

    def two(i, carry):
        layer_two(i)
        return carry

    bands = height // PATCH
    per_band = PATCH // 16
    blocks = height // 16
    sends = []
    done = 0
    for band in range(bands):
        upto = min((band + 1) * per_band + 1, blocks)
        lax.fori_loop(done, upto, one, 0)
        done = upto
        if band == 0:

            @pl.when(gy == 0)
            def _():
                hidden[0, :, :] = jnp.zeros((3 * CH, width), BF16)

        if band == bands - 1:
            layer_one(blocks, 2)

            @pl.when(gy == n_gy - 1)
            def _():
                hidden[height + 1, :, :] = jnp.zeros((3 * CH, width), BF16)

        lax.fori_loop(band * per_band, (band + 1) * per_band, two, 0)
        sends.append(
            pltpu.make_async_remote_copy(
                src_ref=own.at[pl.ds(band * PATCH, PATCH), :],
                dst_ref=following.at[pl.ds(band * PATCH, PATCH), :],
                send_sem=next_send.at[band],
                recv_sem=next_recv.at[band],
                device_id=device(-1, 0, 0),
                device_id_type=MESH,
            )
        )

        @pl.when(not_first)
        def _():
            sends[band].start()

    @pl.when(not_last)
    def _():
        table = table_ref[...]
        spectra = [spectrum(own[band * PATCH : (band + 1) * PATCH, :], table) for band in range(bands)]
        for band in range(bands):
            sends[band].wait_recv()
            real, imag = spectra[band]
            other_real, other_imag = spectrum(following[band * PATCH : (band + 1) * PATCH, :], table)
            rows = slice(band * PATCH, (band + 1) * PATCH)
            out_ref[0, 0, rows, :] = real * other_real + imag * other_imag
            out_ref[0, 1, rows, :] = imag * other_real - real * other_imag

    @pl.when(jnp.logical_not(not_last))
    def _():
        out_ref[...] = jnp.zeros(out_ref.shape, F32)

    for n, (dy, dx) in enumerate(STEPS):

        @pl.when(present(dy, dx))
        def _():
            copies[n].wait_send()

    @pl.when(not_first)
    def _():
        for band in range(bands):
            sends[band].wait_send()


def on_device(sizes, section, first_kernel, first_bias, second_kernel, second_bias, head_weight):
    height, width = section.shape[1:]
    bands = height // PATCH
    vmem = pl.BlockSpec(memory_space=pltpu.VMEM)
    smem = pl.BlockSpec(memory_space=pltpu.SMEM)
    return pl.pallas_call(
        functools.partial(body, sizes),
        out_shape=jax.ShapeDtypeStruct((1, 2, height, width), F32),
        in_specs=[vmem] * 4 + [smem] * 3,
        out_specs=vmem,
        scratch_shapes=[
            pltpu.VMEM((height + 2 * EDGE, width + 2 * LANES), BF16),
            pltpu.VMEM((3, height + 2 * EDGE, width + LANES), BF16),
            pltpu.VMEM((height + 16, 3 * CH, width), BF16),
            pltpu.VMEM((height, width), BF16),
            pltpu.VMEM((height, width), BF16),
            pltpu.VMEM((16 * CH, 256), BF16),
            pltpu.VMEM((ROWS_OUT * CH, 512), BF16),
            pltpu.SemaphoreType.DMA((8,)),
            pltpu.SemaphoreType.DMA((8,)),
            pltpu.SemaphoreType.DMA((bands,)),
            pltpu.SemaphoreType.DMA((bands,)),
        ],
        compiler_params=pltpu.CompilerParams(
            collective_id=0, has_side_effects=True, vmem_limit_bytes=48 * 1024 * 1024
        ),
        name="restore_spectra",
    )(section[0], first_kernel, second_kernel, jnp.asarray(dft_table()), first_bias, second_bias, head_weight)


def solution(mesh):
    sizes = tuple(mesh.shape[name] for name in ("gz", "gy", "gx"))
    placed = (P("gz", "gy", "gx"), P(), P(), P(), P(), P())
    return jax.shard_map(
        functools.partial(on_device, sizes),
        mesh=mesh,
        in_specs=placed,
        out_specs=P("gz", None, "gy", "gx"),
        check_vma=False,
    )
```

```python
import functools
import math

import jax
import jax.numpy as jnp
import numpy as np
from jax import lax
from jax.experimental import pallas as pl
from jax.experimental.pallas import tpu as pltpu
from jax.sharding import PartitionSpec as P

PATCH = 128
CH = 16
EDGE = 16
LANES = 128
ROWS_OUT = 8
F32 = jnp.float32
BF16 = jnp.bfloat16
MESH = pl.DeviceIdType.MESH
SHIFT = jnp.bfloat16
STEPS = [(-1, 0), (1, 0), (0, -1), (0, 1), (-1, -1), (-1, 1), (1, -1), (1, 1)]


def dft_table():
    positions = np.arange(PATCH)
    phase = (positions[:, None] * positions[None, :]) % PATCH
    angles = phase * (2.0 * math.pi / PATCH)
    both = np.concatenate([np.cos(angles), np.sin(angles)], axis=1) / math.sqrt(PATCH)
    return both.astype(np.float32)


def iota(shape, dim):
    return lax.broadcasted_iota(jnp.int32, shape, dim)


def dot(a, b):
    return jnp.dot(a, b, preferred_element_type=F32)


def pieces(value, count):
    out = []
    for _ in range(count):
        part = value.astype(BF16)
        out.append(part)
        value = value - part.astype(F32)
    return out


def column_of(ref, ids):
    column = jnp.zeros(ids.shape, F32)
    for c in range(CH):
        column = jnp.where(ids == c, ref[c], column)
    return column


def first_weights(kernel_ref, bias_ref):
    rows, depth = 16 * CH, 256
    high, low = pieces(kernel_ref[...], 2)
    k = iota((9, depth), 1)
    tap = iota((9, depth), 0)
    split, col_off = k // 96, (k % 96) // 32
    m = iota((rows, depth), 0)
    kk = iota((rows, depth), 1)
    spread = jnp.where(iota((rows, CH), 0) % CH == iota((rows, CH), 1), 1.0, 0.0).astype(BF16)
    offset = (kk % 96) % 32 - 14 - m // CH
    weights = jnp.zeros((rows, depth), F32)
    for a in range(3):
        hit = tap == 3 * a + col_off
        placed = dot(high, jnp.where(hit & (split == 0), 1.0, 0.0).astype(BF16))
        placed = placed + dot(low, jnp.where(hit & (split == 1), 1.0, 0.0).astype(BF16))
        weights = jnp.where(offset == a, dot(spread, placed.astype(BF16)), weights)
    parts = pieces(column_of(bias_ref, m % CH), 3)
    weights = jnp.where(kk >= 192, 0.0, weights)
    for n, part in enumerate(parts):
        weights = jnp.where(kk == 192 + n, part.astype(F32), weights)
    return weights.astype(BF16)


def second_weights(kernel_ref, bias_ref):
    rows, depth = ROWS_OUT * CH, 512
    flat = kernel_ref[...].reshape(9 * CH, CH)
    tile = jnp.where(iota((CH, depth), 1) % CH == iota((CH, depth), 0), 1.0, 0.0).astype(BF16)
    tiled = dot(flat, tile).astype(BF16)
    spread = jnp.where(iota((rows, CH), 0) // ROWS_OUT == iota((rows, CH), 1), 1.0, 0.0).astype(BF16)
    m = iota((rows, depth), 0)
    kk = iota((rows, depth), 1)
    slot = kk // CH - 3 * (m % ROWS_OUT)
    weights = jnp.zeros((rows, depth), F32)
    for t in range(9):
        weights = jnp.where(slot == t, dot(spread, tiled[t * CH : (t + 1) * CH]), weights)
    parts = pieces(column_of(bias_ref, m // ROWS_OUT), 3)
    weights = jnp.where(kk >= 480, 0.0, weights)
    for n, part in enumerate(parts):
        weights = jnp.where(kk == 480 + n, part.astype(F32), weights)
    return weights.astype(BF16)


def spectrum(image, table):
    cosine, sine = table[:, :PATCH], table[:, PATCH:]
    patches = image.shape[1] // PATCH
    stacked = jnp.concatenate([image[:, n * PATCH : (n + 1) * PATCH] for n in range(patches)], axis=0)
    rows = dot(stacked, table).astype(BF16)
    parts = [rows[n * PATCH : (n + 1) * PATCH] for n in range(patches)]
    lower = jnp.concatenate(
        [
            jnp.concatenate([p[:, :PATCH] for p in parts], axis=1),
            jnp.concatenate([p[:, PATCH:] for p in parts], axis=1),
        ],
        axis=0,
    )
    full = jnp.concatenate(
        [jnp.concatenate([cosine, -sine], axis=1), jnp.concatenate([-sine, -cosine], axis=1)], axis=0
    )
    both = dot(full, lower)
    return both[:PATCH], both[PATCH:]


def body(
    sizes,
    x_hbm, k1_hbm, k2_hbm, table_hbm, b1_hbm, b2_hbm, hw_hbm,
    out_ref,
    x_ref, k1_ref, k2_ref, table_ref, b1_ref, b2_ref, hw_ref,
    halo, shifted, hidden, own, following, w1_ref, w2_ref,
    halo_send, halo_recv, next_send, next_recv, local_sem,
):
    n_gz, n_gy, n_gx = sizes
    height, width = x_ref.shape
    wide = width + LANES
    near = [k1_ref, b1_ref, k2_ref, b2_ref, x_ref, hw_ref, table_ref]
    far = [k1_hbm, b1_hbm, k2_hbm, b2_hbm, x_hbm, hw_hbm, table_hbm]
    loads = [
        pltpu.make_async_copy(source, target, local_sem.at[n])
        for n, (source, target) in enumerate(zip(far, near))
    ]
    for load in loads:
        load.start()
    gz, gy, gx = lax.axis_index("gz"), lax.axis_index("gy"), lax.axis_index("gx")

    def present(dy, dx):
        y, x = gy + dy, gx + dx
        return (y >= 0) & (y < n_gy) & (x >= 0) & (x < n_gx)

    def device(dz, dy, dx):
        return (
            lax.rem(gz + dz + n_gz, n_gz),
            lax.rem(gy + dy + n_gy, n_gy),
            lax.rem(gx + dx + n_gx, n_gx),
        )

    not_first, not_last = gz > 0, gz < n_gz - 1

    barrier = pltpu.get_barrier_semaphore()
    count = not_first.astype(jnp.int32) + not_last.astype(jnp.int32)
    for dy, dx in STEPS:
        count = count + present(dy, dx).astype(jnp.int32)

        @pl.when(present(dy, dx))
        def _():
            pl.semaphore_signal(barrier, inc=1, device_id=device(0, dy, dx), device_id_type=MESH)

    @pl.when(not_first)
    def _():
        pl.semaphore_signal(barrier, inc=1, device_id=device(-1, 0, 0), device_id_type=MESH)

    @pl.when(not_last)
    def _():
        pl.semaphore_signal(barrier, inc=1, device_id=device(1, 0, 0), device_id_type=MESH)

    pl.semaphore_wait(barrier, count)

    row_src = {-1: (0, EDGE), 1: (height - EDGE, EDGE), 0: (0, height)}
    col_src = {-1: (0, LANES), 1: (width - LANES, LANES), 0: (0, width)}
    row_dst = {-1: EDGE + height, 1: 0, 0: EDGE}
    col_dst = {-1: width, 1: width + LANES, 0: 0}
    copies = []
    for n, (dy, dx) in enumerate(STEPS):
        (r0, rn), (c0, cn) = row_src[dy], col_src[dx]
        copies.append(
            pltpu.make_async_remote_copy(
                src_ref=x_hbm.at[pl.ds(r0, rn), pl.ds(c0, cn)],
                dst_ref=halo.at[pl.ds(row_dst[dy], rn), pl.ds(col_dst[dx], cn)],
                send_sem=halo_send.at[n],
                recv_sem=halo_recv.at[n],
                device_id=device(0, dy, dx),
                device_id_type=MESH,
            )
        )
    for n, (dy, dx) in enumerate(STEPS):

        @pl.when(present(dy, dx))
        def _():
            copies[n].start()

        @pl.when(jnp.logical_not(present(-dy, -dx)))
        def _():
            rn, cn = row_src[dy][1], col_src[dx][1]
            halo[pl.ds(row_dst[dy], rn), pl.ds(col_dst[dx], cn)] = jnp.zeros((rn, cn), BF16)

    loads[0].wait()
    loads[1].wait()
    w1_ref[...] = first_weights(k1_ref, b1_ref)
    loads[2].wait()
    loads[3].wait()
    w2_ref[...] = second_weights(k2_ref, b2_ref)
    for load in loads[4:]:
        load.wait()

    for n, (dy, dx) in enumerate(STEPS):

        @pl.when(present(-dy, -dx))
        def _():
            copies[n].wait_recv()

    def shift(blocks, step, before, after):
        lane = iota(blocks[0].shape, 1)
        rolled = [pltpu.roll(block, step % LANES, 1) for block in blocks]
        if step > 0:
            fill = [before] + rolled[:-1]
            return [jnp.where(lane == 0, f, r) for f, r in zip(fill, rolled)]
        fill = rolled[1:] + [after]
        return [jnp.where(lane == LANES - 1, f, r) for f, r in zip(fill, rolled)]

    def place(row, size, centre):
        lane = iota((size, LANES), 1)
        right = halo[row : row + size, width : width + LANES].astype(F32)
        left = halo[row : row + size, width + LANES : width + 2 * LANES].astype(F32)
        blocks = [centre[:, n : n + LANES].astype(F32) for n in range(0, width, LANES)]
        left_1, right_1 = pltpu.roll(left, 1, 1), pltpu.roll(right, LANES - 1, 1)
        taps = [
            shift(blocks, 1, left_1, None)
            + [jnp.where(lane == LANES - 1, blocks[-1], pltpu.roll(left, 2, 1))],
            blocks + [jnp.where(lane == LANES - 1, right_1, left_1)],
            shift(blocks, -1, None, right_1)
            + [jnp.where(lane == LANES - 1, pltpu.roll(right, LANES - 2, 1), blocks[0])],
        ]
        for b in range(3):
            shifted[b, row : row + size, :] = jnp.concatenate(taps[b], axis=1).astype(BF16)

    place(0, EDGE, halo[0:EDGE, 0:width])
    for row in range(0, height, 64):
        place(EDGE + row, 64, x_ref[row : row + 64, :])
    place(EDGE + height, EDGE, halo[EDGE + height : 2 * EDGE + height, 0:width])

    lane = iota((1, LANES), 1)
    keep = ((lane == 0) & (gx > 0)) | ((lane == LANES - 1) & (gx < n_gx - 1))
    keep = jnp.where(keep, 1.0, 0.0)

    def layer_one(i, rows):
        start = i * 16
        taps = [shifted[b, start : start + 32, :] for b in range(3)]
        stack = jnp.concatenate(taps + taps + [jnp.ones((16, wide), BF16)], axis=0)
        value = jnp.maximum(dot(w1_ref[0 : rows * CH, 0:208], stack), 0.0)
        outer = (value[:, width:] * keep).astype(SHIFT)
        blocks = [value[:, n : n + LANES].astype(SHIFT) for n in range(0, width, LANES)]
        for b, part in enumerate([shift(blocks, 1, outer, None), blocks, shift(blocks, -1, None, outer)]):
            hidden[start : start + rows, b * CH : (b + 1) * CH, :] = (
                jnp.concatenate(part, axis=1).astype(BF16).reshape(rows, CH, width)
            )

    def layer_two(i):
        start = i * 16
        rows = []
        for g in range(2):
            first = start + g * ROWS_OUT
            window = hidden[first : first + ROWS_OUT + 2, :, :].reshape(480, width)
            stack = jnp.concatenate([window, jnp.ones((16, width), BF16)], axis=0)
            deep = jnp.maximum(dot(w2_ref[:, 0:496], stack), 0.0)
            total = hw_ref[0] * deep[0:ROWS_OUT]
            for o in range(1, CH):
                total = total + hw_ref[o] * deep[o * ROWS_OUT : (o + 1) * ROWS_OUT]
            rows.append(total)
        total = jnp.concatenate(rows, axis=0)
        own[start : start + 16, :] = (x_ref[start : start + 16, :].astype(F32) + total).astype(BF16)

    bands = height // PATCH
    per_band = PATCH // 16
    blocks = height // 16
    sends = []
    done = 0
    for band in range(bands):
        upto = min((band + 1) * per_band + 1, blocks)
        for i in range(done, upto):
            layer_one(i, 16)
        done = upto
        if band == 0:

            @pl.when(gy == 0)
            def _():
                hidden[0, :, :] = jnp.zeros((3 * CH, width), BF16)

        if band == bands - 1:
            layer_one(blocks, 2)

            @pl.when(gy == n_gy - 1)
            def _():
                hidden[height + 1, :, :] = jnp.zeros((3 * CH, width), BF16)

        for i in range(band * per_band, (band + 1) * per_band):
            layer_two(i)
        sends.append(
            pltpu.make_async_remote_copy(
                src_ref=own.at[pl.ds(band * PATCH, PATCH), :],
                dst_ref=following.at[pl.ds(band * PATCH, PATCH), :],
                send_sem=next_send.at[band],
                recv_sem=next_recv.at[band],
                device_id=device(-1, 0, 0),
                device_id_type=MESH,
            )
        )

        @pl.when(not_first)
        def _():
            sends[band].start()

    @pl.when(not_last)
    def _():
        table = table_ref[...].astype(BF16)
        spectra = [spectrum(own[band * PATCH : (band + 1) * PATCH, :], table) for band in range(bands)]
        for band in range(bands):
            sends[band].wait_recv()
            real, imag = spectra[band]
            other_real, other_imag = spectrum(following[band * PATCH : (band + 1) * PATCH, :], table)
            rows = slice(band * PATCH, (band + 1) * PATCH)
            out_ref[0, 0, rows, :] = real * other_real + imag * other_imag
            out_ref[0, 1, rows, :] = imag * other_real - real * other_imag

    @pl.when(jnp.logical_not(not_last))
    def _():
        out_ref[...] = jnp.zeros(out_ref.shape, F32)

    for n, (dy, dx) in enumerate(STEPS):

        @pl.when(present(dy, dx))
        def _():
            copies[n].wait_send()

    @pl.when(not_first)
    def _():
        for band in range(bands):
            sends[band].wait_send()


def on_device(sizes, section, first_kernel, first_bias, second_kernel, second_bias, head_weight):
    height, width = section.shape[1:]
    bands = height // PATCH
    vmem = pl.BlockSpec(memory_space=pltpu.VMEM)
    hbm = pl.BlockSpec(memory_space=pltpu.HBM)
    return pl.pallas_call(
        functools.partial(body, sizes),
        out_shape=jax.ShapeDtypeStruct((1, 2, height, width), F32),
        in_specs=[hbm] * 7,
        out_specs=vmem,
        scratch_shapes=[
            pltpu.VMEM((height, width), BF16),
            pltpu.VMEM(first_kernel.shape, F32),
            pltpu.VMEM(second_kernel.shape, BF16),
            pltpu.VMEM((PATCH, 2 * PATCH), F32),
            pltpu.SMEM((CH,), F32),
            pltpu.SMEM((CH,), F32),
            pltpu.SMEM((CH,), F32),
            pltpu.VMEM((height + 2 * EDGE, width + 2 * LANES), BF16),
            pltpu.VMEM((3, height + 2 * EDGE, width + LANES), BF16),
            pltpu.VMEM((height + 16, 3 * CH, width), BF16),
            pltpu.VMEM((height, width), BF16),
            pltpu.VMEM((height, width), BF16),
            pltpu.VMEM((16 * CH, 256), BF16),
            pltpu.VMEM((ROWS_OUT * CH, 512), BF16),
            pltpu.SemaphoreType.DMA((8,)),
            pltpu.SemaphoreType.DMA((8,)),
            pltpu.SemaphoreType.DMA((bands,)),
            pltpu.SemaphoreType.DMA((bands,)),
            pltpu.SemaphoreType.DMA((7,)),
        ],
        compiler_params=pltpu.CompilerParams(
            collective_id=0, has_side_effects=True, vmem_limit_bytes=48 * 1024 * 1024
        ),
        name="restore_spectra",
    )(section[0], first_kernel, second_kernel, jnp.asarray(dft_table()), first_bias, second_bias, head_weight)


def solution(mesh):
    sizes = tuple(mesh.shape[name] for name in ("gz", "gy", "gx"))
    placed = (P("gz", "gy", "gx"), P(), P(), P(), P(), P())
    return jax.shard_map(
        functools.partial(on_device, sizes),
        mesh=mesh,
        in_specs=placed,
        out_specs=P("gz", None, "gy", "gx"),
        check_vma=False,
    )
```

```python
import functools
import math

import jax
import jax.numpy as jnp
import numpy as np
from jax import lax
from jax.experimental import pallas as pl
from jax.experimental.pallas import tpu as pltpu
from jax.sharding import PartitionSpec as P

PATCH = 128
CH = 16
EDGE = 16
LANES = 128
ROWS_OUT = 8
F32 = jnp.float32
BF16 = jnp.bfloat16
MESH = pl.DeviceIdType.MESH
SHIFT = jnp.bfloat16
STEPS = [(-1, 0), (1, 0), (0, -1), (0, 1), (-1, -1), (-1, 1), (1, -1), (1, 1)]


def dft_table():
    positions = np.arange(PATCH)
    phase = (positions[:, None] * positions[None, :]) % PATCH
    angles = phase * (2.0 * math.pi / PATCH)
    both = np.concatenate([np.cos(angles), np.sin(angles)], axis=1) / math.sqrt(PATCH)
    return both.astype(np.float32)


def iota(shape, dim):
    return lax.broadcasted_iota(jnp.int32, shape, dim)


def dot(a, b):
    return jnp.dot(a, b, preferred_element_type=F32)


def pieces(value, count):
    out = []
    for _ in range(count):
        part = value.astype(BF16)
        out.append(part)
        value = value - part.astype(F32)
    return out


def column_of(ref):
    ids = iota((CH, 1), 0)
    column = jnp.zeros((CH, 1), F32)
    for c in range(CH):
        column = jnp.where(ids == c, ref[c], column)
    return column


def one_hot(hit):
    return jnp.where(hit, 1.0, 0.0).astype(BF16)


def with_bias(values, ref, lanes, first):
    for n, part in enumerate(pieces(column_of(ref), 3)):
        values = jnp.where(lanes == first + n, part.astype(F32), values)
    return values


def first_weights(kernel_ref, bias_ref):
    rows, depth = 16 * CH, 256
    high, low = pieces(kernel_ref[...], 2)
    k = iota((9, depth), 1)
    tap = iota((9, depth), 0)
    col_off = (k & 127) >> 5
    lanes = iota((CH, depth), 1)
    m = iota((rows, depth), 0)
    kk = iota((rows, depth), 1)
    spread = one_hot((iota((rows, CH), 0) & (CH - 1)) == iota((rows, CH), 1))
    fixed = (kk & 127) >= 96
    offset = (kk & 31) - 14 - (m >> 4)
    weights = jnp.zeros((rows, depth), F32)
    for a in range(3):
        hit = (tap == 3 * a + col_off) & (col_off < 3)
        placed = dot(high, one_hot(hit & (k < 128))) + dot(low, one_hot(hit & (k >= 128)))
        placed = with_bias(placed, bias_ref, lanes, 96)
        weights = jnp.where(fixed | (offset == a), dot(spread, placed.astype(BF16)), weights)
    return weights.astype(BF16)


def second_weights(kernel_ref, bias_ref):
    rows, depth = ROWS_OUT * CH, 512
    flat = kernel_ref[...].reshape(9 * CH, CH)
    tiled = dot(flat, one_hot((iota((CH, depth), 1) & (CH - 1)) == iota((CH, depth), 0))).astype(BF16)
    spread = one_hot((iota((rows, CH), 0) >> 3) == iota((rows, CH), 1))
    slot = (iota((rows, depth), 1) >> 4) - 3 * (iota((rows, depth), 0) & (ROWS_OUT - 1))
    weights = jnp.zeros((rows, depth), F32)
    for t in range(9):
        weights = jnp.where(slot == t, dot(spread, tiled[t * CH : (t + 1) * CH]), weights)
    lanes = iota((CH, LANES), 1)
    bias = with_bias(jnp.zeros((CH, LANES), F32), bias_ref, lanes, 96)
    tail = jnp.where(iota((rows, LANES), 1) >= 96, dot(spread, bias.astype(BF16)), weights[:, 384:])
    return jnp.concatenate([weights[:, :384], tail], axis=1).astype(BF16)


def spectrum(image, table):
    cosine, sine = table[:, :PATCH], table[:, PATCH:]
    patches = image.shape[1] // PATCH
    stacked = jnp.concatenate([image[:, n * PATCH : (n + 1) * PATCH] for n in range(patches)], axis=0)
    rows = dot(stacked, table).astype(BF16)
    parts = [rows[n * PATCH : (n + 1) * PATCH] for n in range(patches)]
    lower = jnp.concatenate(
        [
            jnp.concatenate([p[:, :PATCH] for p in parts], axis=1),
            jnp.concatenate([p[:, PATCH:] for p in parts], axis=1),
        ],
        axis=0,
    )
    full = jnp.concatenate(
        [jnp.concatenate([cosine, -sine], axis=1), jnp.concatenate([-sine, -cosine], axis=1)], axis=0
    )
    both = dot(full, lower)
    return both[:PATCH], both[PATCH:]


def chunk_bounds(height):
    return list(range(0, height - PATCH + 1, PATCH)) + [height - PATCH // 2, height - PATCH // 4, height]


def body(
    sizes,
    x_hbm, k1_hbm, k2_hbm, table_hbm, b1_hbm, b2_hbm, hw_hbm,
    out_hbm,
    x_ref, k1_ref, k2_ref, table_ref, b1_ref, b2_ref, hw_ref,
    halo, shifted, hidden, own, following, w1_ref, w2_ref,
    halo_send, halo_recv, next_send, next_recv, local_sem, out_ref, out_sem,
):
    n_gz, n_gy, n_gx = sizes
    height, width = x_ref.shape
    wide = width + LANES
    near = [k1_ref, b1_ref, k2_ref, b2_ref, x_ref, hw_ref, table_ref]
    far = [k1_hbm, b1_hbm, k2_hbm, b2_hbm, x_hbm, hw_hbm, table_hbm]
    loads = [
        pltpu.make_async_copy(source, target, local_sem.at[n])
        for n, (source, target) in enumerate(zip(far, near))
    ]
    for load in loads:
        load.start()
    gz, gy, gx = lax.axis_index("gz"), lax.axis_index("gy"), lax.axis_index("gx")

    def present(dy, dx):
        y, x = gy + dy, gx + dx
        return (y >= 0) & (y < n_gy) & (x >= 0) & (x < n_gx)

    def device(dz, dy, dx):
        return (
            lax.rem(gz + dz + n_gz, n_gz),
            lax.rem(gy + dy + n_gy, n_gy),
            lax.rem(gx + dx + n_gx, n_gx),
        )

    not_first, not_last = gz > 0, gz < n_gz - 1

    barrier = pltpu.get_barrier_semaphore()
    count = not_first.astype(jnp.int32) + not_last.astype(jnp.int32)
    for dy, dx in STEPS:
        count = count + present(dy, dx).astype(jnp.int32)

        @pl.when(present(dy, dx))
        def _():
            pl.semaphore_signal(barrier, inc=1, device_id=device(0, dy, dx), device_id_type=MESH)

    @pl.when(not_first)
    def _():
        pl.semaphore_signal(barrier, inc=1, device_id=device(-1, 0, 0), device_id_type=MESH)

    @pl.when(not_last)
    def _():
        pl.semaphore_signal(barrier, inc=1, device_id=device(1, 0, 0), device_id_type=MESH)

    pl.semaphore_wait(barrier, count)

    row_src = {-1: (0, EDGE), 1: (height - EDGE, EDGE), 0: (0, height)}
    col_src = {-1: (0, LANES), 1: (width - LANES, LANES), 0: (0, width)}
    row_dst = {-1: EDGE + height, 1: 0, 0: EDGE}
    col_dst = {-1: width, 1: width + LANES, 0: 0}
    copies = []
    for n, (dy, dx) in enumerate(STEPS):
        (r0, rn), (c0, cn) = row_src[dy], col_src[dx]
        copies.append(
            pltpu.make_async_remote_copy(
                src_ref=x_hbm.at[pl.ds(r0, rn), pl.ds(c0, cn)],
                dst_ref=halo.at[pl.ds(row_dst[dy], rn), pl.ds(col_dst[dx], cn)],
                send_sem=halo_send.at[n],
                recv_sem=halo_recv.at[n],
                device_id=device(0, dy, dx),
                device_id_type=MESH,
            )
        )
    for n, (dy, dx) in enumerate(STEPS):

        @pl.when(present(dy, dx))
        def _():
            copies[n].start()

        @pl.when(jnp.logical_not(present(-dy, -dx)))
        def _():
            rn, cn = row_src[dy][1], col_src[dx][1]
            halo[pl.ds(row_dst[dy], rn), pl.ds(col_dst[dx], cn)] = jnp.zeros((rn, cn), BF16)

    loads[0].wait()
    loads[1].wait()
    w1_ref[...] = first_weights(k1_ref, b1_ref)
    loads[2].wait()
    loads[3].wait()
    w2_ref[...] = second_weights(k2_ref, b2_ref)
    for load in loads[4:]:
        load.wait()

    def receive(chosen):
        for n in chosen:
            dy, dx = STEPS[n]

            @pl.when(present(-dy, -dx))
            def _():
                copies[n].wait_recv()

    def shift(blocks, step, before, after):
        lane = iota(blocks[0].shape, 1)
        rolled = [pltpu.roll(block, step % LANES, 1) for block in blocks]
        if step > 0:
            fill = [before] + rolled[:-1]
            return [jnp.where(lane == 0, f, r) for f, r in zip(fill, rolled)]
        fill = rolled[1:] + [after]
        return [jnp.where(lane == LANES - 1, f, r) for f, r in zip(fill, rolled)]

    def place(row, size, centre):
        lane = iota((size, LANES), 1)
        right = halo[row : row + size, width : width + LANES]
        left = halo[row : row + size, width + LANES : width + 2 * LANES]
        blocks = [centre[:, n : n + LANES] for n in range(0, width, LANES)]
        left_1, right_1 = pltpu.roll(left, 1, 1), pltpu.roll(right, LANES - 1, 1)
        taps = [
            shift(blocks, 1, left_1, None)
            + [jnp.where(lane == LANES - 1, blocks[-1], pltpu.roll(left, 2, 1))],
            blocks + [jnp.where(lane == LANES - 1, right_1, left_1)],
            shift(blocks, -1, None, right_1)
            + [jnp.where(lane == LANES - 1, pltpu.roll(right, LANES - 2, 1), blocks[0])],
        ]
        for b in range(3):
            shifted[b, row : row + size, :] = jnp.concatenate(taps[b], axis=1)

    def place_edges():
        place(0, EDGE, halo[0:EDGE, 0:width])
        place(EDGE + height, EDGE, halo[EDGE + height : 2 * EDGE + height, 0:width])

    receive((2, 3))
    for row in range(0, height, 64):
        place(EDGE + row, 64, x_ref[row : row + 64, :])

    lane = iota((1, LANES), 1)
    keep = ((lane == 0) & (gx > 0)) | ((lane == LANES - 1) & (gx < n_gx - 1))
    keep = jnp.where(keep, 1.0, 0.0)
    above = jnp.where(gy > 0, 1.0, 0.0)
    below = jnp.where(gy < n_gy - 1, 1.0, 0.0)
    blocks_16 = height // 16

    def layer_one(i, rows):
        start = i * 16
        taps = [shifted[b, start : start + 32, :] for b in range(3)]
        stack = jnp.concatenate(taps + [jnp.ones((32, wide), BF16)] + taps, axis=0)
        value = jnp.maximum(dot(w1_ref[0 : rows * CH, 0:224], stack), 0.0)
        if i == 0:
            value = jnp.concatenate([value[:CH] * above, value[CH:]], axis=0)
        if i == blocks_16:
            value = jnp.concatenate([value[:CH], value[CH : 2 * CH] * below], axis=0)
        outer = (value[:, width:] * keep).astype(SHIFT)
        blocks = [value[:, n : n + LANES].astype(SHIFT) for n in range(0, width, LANES)]
        for b, part in enumerate([shift(blocks, 1, outer, None), blocks, shift(blocks, -1, None, outer)]):
            hidden[start : start + rows, b * CH : (b + 1) * CH, :] = (
                jnp.concatenate(part, axis=1).astype(BF16).reshape(rows, CH, width)
            )

    def layer_two(i):
        start = i * 16
        rows = []
        for g in range(2):
            first = start + g * ROWS_OUT
            window = hidden[first : first + ROWS_OUT + 2, :, :].reshape(480, width)
            stack = jnp.concatenate([window, jnp.ones((16, width), BF16)], axis=0)
            deep = jnp.maximum(dot(w2_ref[:, 0:496], stack), 0.0)
            total = hw_ref[0] * deep[0:ROWS_OUT]
            for o in range(1, CH):
                total = total + hw_ref[o] * deep[o * ROWS_OUT : (o + 1) * ROWS_OUT]
            rows.append(total)
        total = jnp.concatenate(rows, axis=0)
        own[start : start + 16, :] = (x_ref[start : start + 16, :].astype(F32) + total).astype(BF16)

    bands = height // PATCH
    bounds = chunk_bounds(height)
    sends = []
    for n in range(len(bounds) - 1):
        rows = pl.ds(bounds[n], bounds[n + 1] - bounds[n])
        sends.append(
            pltpu.make_async_remote_copy(
                src_ref=own.at[rows, :],
                dst_ref=following.at[rows, :],
                send_sem=next_send.at[n],
                recv_sem=next_recv.at[n],
                device_id=device(-1, 0, 0),
                device_id_type=MESH,
            )
        )

    ahead = 4
    for i in range(1, ahead):
        layer_one(i, 16)
    receive((0, 1, 4, 5, 6, 7))
    place_edges()
    layer_one(0, 16)
    for i in range(blocks_16):
        j = i + ahead
        if j < blocks_16:
            layer_one(j, 16)
        elif j == blocks_16:
            layer_one(j, 2)
        layer_two(i)
        if (i + 1) * 16 in bounds:

            @pl.when(not_first)
            def _():
                sends[bounds.index((i + 1) * 16) - 1].start()

    outs = [
        pltpu.make_async_copy(
            out_ref.at[:, pl.ds(band * PATCH, PATCH), :],
            out_hbm.at[0, :, pl.ds(band * PATCH, PATCH), :],
            out_sem.at[band],
        )
        for band in range(bands)
    ]

    @pl.when(not_last)
    def _():
        table = table_ref[...].astype(BF16)
        spectra = [spectrum(own[band * PATCH : (band + 1) * PATCH, :], table) for band in range(bands)]
        for band in range(bands):
            for n in range(len(sends)):
                if band * PATCH < bounds[n + 1] <= (band + 1) * PATCH:
                    sends[n].wait_recv()
            real, imag = spectra[band]
            other_real, other_imag = spectrum(following[band * PATCH : (band + 1) * PATCH, :], table)
            rows = slice(band * PATCH, (band + 1) * PATCH)
            out_ref[0, rows, :] = real * other_real + imag * other_imag
            out_ref[1, rows, :] = imag * other_real - real * other_imag
            outs[band].start()

    @pl.when(jnp.logical_not(not_last))
    def _():
        out_ref[...] = jnp.zeros(out_ref.shape, F32)
        for out in outs:
            out.start()

    for n, (dy, dx) in enumerate(STEPS):

        @pl.when(present(dy, dx))
        def _():
            copies[n].wait_send()

    @pl.when(not_first)
    def _():
        for send in sends:
            send.wait_send()

    for out in outs:
        out.wait()


def on_device(sizes, section, first_kernel, first_bias, second_kernel, second_bias, head_weight):
    height, width = section.shape[1:]
    bands = height // PATCH
    chunks = len(chunk_bounds(height)) - 1
    hbm = pl.BlockSpec(memory_space=pltpu.HBM)
    return pl.pallas_call(
        functools.partial(body, sizes),
        out_shape=jax.ShapeDtypeStruct((1, 2, height, width), F32),
        in_specs=[hbm] * 7,
        out_specs=hbm,
        scratch_shapes=[
            pltpu.VMEM((height, width), BF16),
            pltpu.VMEM(first_kernel.shape, F32),
            pltpu.VMEM(second_kernel.shape, BF16),
            pltpu.VMEM((PATCH, 2 * PATCH), F32),
            pltpu.SMEM((CH,), F32),
            pltpu.SMEM((CH,), F32),
            pltpu.SMEM((CH,), F32),
            pltpu.VMEM((height + 2 * EDGE, width + 2 * LANES), BF16),
            pltpu.VMEM((3, height + 2 * EDGE, width + LANES), BF16),
            pltpu.VMEM((height + 16, 3 * CH, width), BF16),
            pltpu.VMEM((height, width), BF16),
            pltpu.VMEM((height, width), BF16),
            pltpu.VMEM((16 * CH, 256), BF16),
            pltpu.VMEM((ROWS_OUT * CH, 512), BF16),
            pltpu.SemaphoreType.DMA((8,)),
            pltpu.SemaphoreType.DMA((8,)),
            pltpu.SemaphoreType.DMA((chunks,)),
            pltpu.SemaphoreType.DMA((chunks,)),
            pltpu.SemaphoreType.DMA((7,)),
            pltpu.VMEM((2, height, width), F32),
            pltpu.SemaphoreType.DMA((bands,)),
        ],
        compiler_params=pltpu.CompilerParams(
            collective_id=0, has_side_effects=True, vmem_limit_bytes=64 * 1024 * 1024
        ),
        name="restore_spectra",
    )(section[0], first_kernel, second_kernel, jnp.asarray(dft_table()), first_bias, second_bias, head_weight)


def solution(mesh):
    sizes = tuple(mesh.shape[name] for name in ("gz", "gy", "gx"))
    placed = (P("gz", "gy", "gx"), P(), P(), P(), P(), P())
    return jax.shard_map(
        functools.partial(on_device, sizes),
        mesh=mesh,
        in_specs=placed,
        out_specs=P("gz", None, "gy", "gx"),
        check_vma=False,
    )
```

```python
import functools
import math

import jax
import jax.numpy as jnp
import numpy as np
from jax import lax
from jax.experimental import pallas as pl
from jax.experimental.pallas import tpu as pltpu
from jax.sharding import PartitionSpec as P

PATCH = 128
CH = 16
EDGE = 16
LANES = 128
ROWS_OUT = 8
F32 = jnp.float32
BF16 = jnp.bfloat16
MESH = pl.DeviceIdType.MESH
SHIFT = jnp.bfloat16
STEPS = [(-1, 0), (1, 0), (0, -1), (0, 1), (-1, -1), (-1, 1), (1, -1), (1, 1)]


def dft_table():
    positions = np.arange(PATCH)
    phase = (positions[:, None] * positions[None, :]) % PATCH
    angles = phase * (2.0 * math.pi / PATCH)
    both = np.concatenate([np.cos(angles), np.sin(angles)], axis=1) / math.sqrt(PATCH)
    return both.astype(np.float32)


def iota(shape, dim):
    return lax.broadcasted_iota(jnp.int32, shape, dim)


def dot(a, b):
    return jnp.dot(a, b, preferred_element_type=F32)


def pieces(value, count):
    out = []
    for _ in range(count):
        part = value.astype(BF16)
        out.append(part)
        value = value - part.astype(F32)
    return out


def column_of(ref):
    ids = iota((CH, 1), 0)
    column = jnp.zeros((CH, 1), F32)
    for c in range(CH):
        column = jnp.where(ids == c, ref[c], column)
    return column


def one_hot(hit):
    return jnp.where(hit, 1.0, 0.0).astype(BF16)


def with_bias(values, ref, lanes, first):
    for n, part in enumerate(pieces(column_of(ref), 3)):
        values = jnp.where(lanes == first + n, part.astype(F32), values)
    return values


def first_weights(kernel_ref, bias_ref):
    rows, depth = 16 * CH, 256
    high, low = pieces(kernel_ref[...], 2)
    k = iota((9, depth), 1)
    tap = iota((9, depth), 0)
    col_off = (k & 127) >> 5
    lanes = iota((CH, depth), 1)
    m = iota((rows, depth), 0)
    kk = iota((rows, depth), 1)
    spread = one_hot((iota((rows, CH), 0) & (CH - 1)) == iota((rows, CH), 1))
    fixed = (kk & 127) >= 96
    offset = (kk & 31) - 14 - (m >> 4)
    weights = jnp.zeros((rows, depth), F32)
    for a in range(3):
        hit = (tap == 3 * a + col_off) & (col_off < 3)
        placed = dot(high, one_hot(hit & (k < 128))) + dot(low, one_hot(hit & (k >= 128)))
        placed = with_bias(placed, bias_ref, lanes, 96)
        weights = jnp.where(fixed | (offset == a), dot(spread, placed.astype(BF16)), weights)
    return weights.astype(BF16)


def second_weights(kernel_ref, bias_ref):
    rows, depth = ROWS_OUT * CH, 512
    flat = kernel_ref[...].reshape(9 * CH, CH)
    tiled = dot(flat, one_hot((iota((CH, depth), 1) & (CH - 1)) == iota((CH, depth), 0))).astype(BF16)
    spread = one_hot((iota((rows, CH), 0) >> 3) == iota((rows, CH), 1))
    slot = (iota((rows, depth), 1) >> 4) - 3 * (iota((rows, depth), 0) & (ROWS_OUT - 1))
    weights = jnp.zeros((rows, depth), F32)
    for t in range(9):
        weights = jnp.where(slot == t, dot(spread, tiled[t * CH : (t + 1) * CH]), weights)
    lanes = iota((CH, LANES), 1)
    bias = with_bias(jnp.zeros((CH, LANES), F32), bias_ref, lanes, 96)
    tail = jnp.where(iota((rows, LANES), 1) >= 96, dot(spread, bias.astype(BF16)), weights[:, 384:])
    return jnp.concatenate([weights[:, :384], tail], axis=1).astype(BF16)


def spectrum(image, table):
    cosine, sine = table[:, :PATCH], table[:, PATCH:]
    patches = image.shape[1] // PATCH
    stacked = jnp.concatenate([image[:, n * PATCH : (n + 1) * PATCH] for n in range(patches)], axis=0)
    rows = dot(stacked, table).astype(BF16)
    parts = [rows[n * PATCH : (n + 1) * PATCH] for n in range(patches)]
    lower = jnp.concatenate(
        [
            jnp.concatenate([p[:, :PATCH] for p in parts], axis=1),
            jnp.concatenate([p[:, PATCH:] for p in parts], axis=1),
        ],
        axis=0,
    )
    full = jnp.concatenate(
        [jnp.concatenate([cosine, -sine], axis=1), jnp.concatenate([-sine, -cosine], axis=1)], axis=0
    )
    both = dot(full, lower)
    return both[:PATCH], both[PATCH:]


def chunk_bounds(height):
    return list(range(0, height - PATCH + 1, PATCH)) + [height - PATCH // 2, height - PATCH // 4, height]


def body(
    sizes,
    x_hbm, k1_hbm, k2_hbm, table_hbm, b1_hbm, b2_hbm, hw_hbm,
    spec_hbm, following,
    x_ref, k1_ref, k2_ref, table_ref, b1_ref, b2_ref, hw_ref,
    halo, shifted, hidden, own, w1_ref, w2_ref,
    halo_send, halo_recv, next_send, next_recv, local_sem, spec_ref, spec_sem,
):
    n_gz, n_gy, n_gx = sizes
    height, width = x_ref.shape
    wide = width + LANES
    near = [k1_ref, b1_ref, k2_ref, b2_ref, x_ref, hw_ref, table_ref]
    far = [k1_hbm, b1_hbm, k2_hbm, b2_hbm, x_hbm, hw_hbm, table_hbm]
    loads = [
        pltpu.make_async_copy(source, target, local_sem.at[n])
        for n, (source, target) in enumerate(zip(far, near))
    ]
    for load in loads:
        load.start()
    gz, gy, gx = lax.axis_index("gz"), lax.axis_index("gy"), lax.axis_index("gx")

    def present(dy, dx):
        y, x = gy + dy, gx + dx
        return (y >= 0) & (y < n_gy) & (x >= 0) & (x < n_gx)

    def device(dz, dy, dx):
        return (
            lax.rem(gz + dz + n_gz, n_gz),
            lax.rem(gy + dy + n_gy, n_gy),
            lax.rem(gx + dx + n_gx, n_gx),
        )

    not_first, not_last = gz > 0, gz < n_gz - 1

    barrier = pltpu.get_barrier_semaphore()
    count = not_first.astype(jnp.int32) + not_last.astype(jnp.int32)
    for dy, dx in STEPS:
        count = count + present(dy, dx).astype(jnp.int32)

        @pl.when(present(dy, dx))
        def _():
            pl.semaphore_signal(barrier, inc=1, device_id=device(0, dy, dx), device_id_type=MESH)

    @pl.when(not_first)
    def _():
        pl.semaphore_signal(barrier, inc=1, device_id=device(-1, 0, 0), device_id_type=MESH)

    @pl.when(not_last)
    def _():
        pl.semaphore_signal(barrier, inc=1, device_id=device(1, 0, 0), device_id_type=MESH)

    pl.semaphore_wait(barrier, count)

    row_src = {-1: (0, EDGE), 1: (height - EDGE, EDGE), 0: (0, height)}
    col_src = {-1: (0, LANES), 1: (width - LANES, LANES), 0: (0, width)}
    row_dst = {-1: EDGE + height, 1: 0, 0: EDGE}
    col_dst = {-1: width, 1: width + LANES, 0: 0}
    copies = []
    for n, (dy, dx) in enumerate(STEPS):
        (r0, rn), (c0, cn) = row_src[dy], col_src[dx]
        copies.append(
            pltpu.make_async_remote_copy(
                src_ref=x_hbm.at[pl.ds(r0, rn), pl.ds(c0, cn)],
                dst_ref=halo.at[pl.ds(row_dst[dy], rn), pl.ds(col_dst[dx], cn)],
                send_sem=halo_send.at[n],
                recv_sem=halo_recv.at[n],
                device_id=device(0, dy, dx),
                device_id_type=MESH,
            )
        )
    for n, (dy, dx) in enumerate(STEPS):

        @pl.when(present(dy, dx))
        def _():
            copies[n].start()

        @pl.when(jnp.logical_not(present(-dy, -dx)))
        def _():
            rn, cn = row_src[dy][1], col_src[dx][1]
            halo[pl.ds(row_dst[dy], rn), pl.ds(col_dst[dx], cn)] = jnp.zeros((rn, cn), BF16)

    loads[0].wait()
    loads[1].wait()
    w1_ref[...] = first_weights(k1_ref, b1_ref)
    loads[2].wait()
    loads[3].wait()
    w2_ref[...] = second_weights(k2_ref, b2_ref)
    for load in loads[4:]:
        load.wait()

    def receive(chosen):
        for n in chosen:
            dy, dx = STEPS[n]

            @pl.when(present(-dy, -dx))
            def _():
                copies[n].wait_recv()

    def shift(blocks, step, before, after):
        lane = iota(blocks[0].shape, 1)
        rolled = [pltpu.roll(block, step % LANES, 1) for block in blocks]
        if step > 0:
            fill = [before] + rolled[:-1]
            return [jnp.where(lane == 0, f, r) for f, r in zip(fill, rolled)]
        fill = rolled[1:] + [after]
        return [jnp.where(lane == LANES - 1, f, r) for f, r in zip(fill, rolled)]

    def place(row, size, centre):
        lane = iota((size, LANES), 1)
        right = halo[row : row + size, width : width + LANES]
        left = halo[row : row + size, width + LANES : width + 2 * LANES]
        blocks = [centre[:, n : n + LANES] for n in range(0, width, LANES)]
        left_1, right_1 = pltpu.roll(left, 1, 1), pltpu.roll(right, LANES - 1, 1)
        taps = [
            shift(blocks, 1, left_1, None)
            + [jnp.where(lane == LANES - 1, blocks[-1], pltpu.roll(left, 2, 1))],
            blocks + [jnp.where(lane == LANES - 1, right_1, left_1)],
            shift(blocks, -1, None, right_1)
            + [jnp.where(lane == LANES - 1, pltpu.roll(right, LANES - 2, 1), blocks[0])],
        ]
        for b in range(3):
            shifted[b, row : row + size, :] = jnp.concatenate(taps[b], axis=1)

    def place_edges():
        place(0, EDGE, halo[0:EDGE, 0:width])
        place(EDGE + height, EDGE, halo[EDGE + height : 2 * EDGE + height, 0:width])

    receive((2, 3))
    for row in range(0, height, 64):
        place(EDGE + row, 64, x_ref[row : row + 64, :])

    lane = iota((1, LANES), 1)
    keep = ((lane == 0) & (gx > 0)) | ((lane == LANES - 1) & (gx < n_gx - 1))
    keep = jnp.where(keep, 1.0, 0.0)
    above = jnp.where(gy > 0, 1.0, 0.0)
    below = jnp.where(gy < n_gy - 1, 1.0, 0.0)
    blocks_16 = height // 16

    def layer_one(i, rows):
        start = i * 16
        taps = [shifted[b, start : start + 32, :] for b in range(3)]
        stack = jnp.concatenate(taps + [jnp.ones((32, wide), BF16)] + taps, axis=0)
        value = jnp.maximum(dot(w1_ref[0 : rows * CH, 0:224], stack), 0.0)
        if i == 0:
            value = jnp.concatenate([value[:CH] * above, value[CH:]], axis=0)
        if i == blocks_16:
            value = jnp.concatenate([value[:CH], value[CH : 2 * CH] * below], axis=0)
        outer = (value[:, width:] * keep).astype(SHIFT)
        blocks = [value[:, n : n + LANES].astype(SHIFT) for n in range(0, width, LANES)]
        for b, part in enumerate([shift(blocks, 1, outer, None), blocks, shift(blocks, -1, None, outer)]):
            hidden[start : start + rows, b * CH : (b + 1) * CH, :] = (
                jnp.concatenate(part, axis=1).astype(BF16).reshape(rows, CH, width)
            )

    def layer_two(i):
        start = i * 16
        rows = []
        for g in range(2):
            first = start + g * ROWS_OUT
            window = hidden[first : first + ROWS_OUT + 2, :, :].reshape(480, width)
            stack = jnp.concatenate([window, jnp.ones((16, width), BF16)], axis=0)
            deep = jnp.maximum(dot(w2_ref[:, 0:496], stack), 0.0)
            total = hw_ref[0] * deep[0:ROWS_OUT]
            for o in range(1, CH):
                total = total + hw_ref[o] * deep[o * ROWS_OUT : (o + 1) * ROWS_OUT]
            rows.append(total)
        total = jnp.concatenate(rows, axis=0)
        own[start : start + 16, :] = (x_ref[start : start + 16, :].astype(F32) + total).astype(BF16)

    bands = height // PATCH
    bounds = chunk_bounds(height)
    sends = []
    for n in range(len(bounds) - 1):
        rows = pl.ds(bounds[n], bounds[n + 1] - bounds[n])
        sends.append(
            pltpu.make_async_remote_copy(
                src_ref=own.at[rows, :],
                dst_ref=following.at[rows, :],
                send_sem=next_send.at[n],
                recv_sem=next_recv.at[n],
                device_id=device(-1, 0, 0),
                device_id_type=MESH,
            )
        )

    stores = [
        pltpu.make_async_copy(
            spec_ref.at[:, pl.ds(band * PATCH, PATCH), :],
            spec_hbm.at[:, pl.ds(band * PATCH, PATCH), :],
            spec_sem.at[band],
        )
        for band in range(bands)
    ]
    table = table_ref[...].astype(BF16)

    ahead = 4
    for i in range(1, ahead):
        layer_one(i, 16)
    receive((0, 1, 4, 5, 6, 7))
    place_edges()
    layer_one(0, 16)
    for i in range(blocks_16):
        j = i + ahead
        if j < blocks_16:
            layer_one(j, 16)
        elif j == blocks_16:
            layer_one(j, 2)
        layer_two(i)
        if (i + 1) * 16 in bounds:

            @pl.when(not_first)
            def _():
                sends[bounds.index((i + 1) * 16) - 1].start()

        if (i + 1) * 16 % PATCH == 0:
            band = i * 16 // PATCH
            rows = slice(band * PATCH, (band + 1) * PATCH)
            spec_ref[0, rows, :], spec_ref[1, rows, :] = spectrum(own[rows, :], table)
            stores[band].start()

    for n, (dy, dx) in enumerate(STEPS):

        @pl.when(present(dy, dx))
        def _():
            copies[n].wait_send()

    @pl.when(not_first)
    def _():
        for send in sends:
            send.wait_send()

    for store in stores:
        store.wait()

    @pl.when(not_last)
    def _():
        for send in sends:
            send.wait_recv()


def cross_body(
    n_gz,
    spec_hbm, following_hbm, table_hbm,
    out_hbm,
    spec, following, table_ref, out_ref, sems, out_sems,
):
    bands = following.shape[0] // PATCH
    not_last = lax.axis_index("gz") < n_gz - 1
    outs = [
        pltpu.make_async_copy(
            out_ref.at[:, pl.ds(band * PATCH, PATCH), :],
            out_hbm.at[0, :, pl.ds(band * PATCH, PATCH), :],
            out_sems.at[band],
        )
        for band in range(bands)
    ]

    @pl.when(not_last)
    def _():
        loads = [pltpu.make_async_copy(table_hbm, table_ref, sems.at[0])]
        for band in range(bands):
            rows = pl.ds(band * PATCH, PATCH)
            loads.append(
                pltpu.make_async_copy(
                    following_hbm.at[rows, :], following.at[rows, :], sems.at[1 + 2 * band]
                )
            )
            loads.append(
                pltpu.make_async_copy(spec_hbm.at[:, rows, :], spec.at[:, rows, :], sems.at[2 + 2 * band])
            )
        for load in loads:
            load.start()
        loads[0].wait()
        table = table_ref[...].astype(BF16)
        for band in range(bands):
            rows = slice(band * PATCH, (band + 1) * PATCH)
            loads[1 + 2 * band].wait()
            other_real, other_imag = spectrum(following[rows, :], table)
            loads[2 + 2 * band].wait()
            real, imag = spec[0, rows, :], spec[1, rows, :]
            out_ref[0, rows, :] = real * other_real + imag * other_imag
            out_ref[1, rows, :] = imag * other_real - real * other_imag
            outs[band].start()

    @pl.when(jnp.logical_not(not_last))
    def _():
        out_ref[...] = jnp.zeros(out_ref.shape, F32)
        for out in outs:
            out.start()

    for out in outs:
        out.wait()


def on_device(sizes, section, first_kernel, first_bias, second_kernel, second_bias, head_weight):
    height, width = section.shape[1:]
    bands = height // PATCH
    chunks = len(chunk_bounds(height)) - 1
    hbm = pl.BlockSpec(memory_space=pltpu.HBM)
    table = jnp.asarray(dft_table())
    spec, following = pl.pallas_call(
        functools.partial(body, sizes),
        out_shape=[
            jax.ShapeDtypeStruct((2, height, width), F32),
            jax.ShapeDtypeStruct((height, width), BF16),
        ],
        in_specs=[hbm] * 7,
        out_specs=[hbm, hbm],
        scratch_shapes=[
            pltpu.VMEM((height, width), BF16),
            pltpu.VMEM(first_kernel.shape, F32),
            pltpu.VMEM(second_kernel.shape, BF16),
            pltpu.VMEM((PATCH, 2 * PATCH), F32),
            pltpu.SMEM((CH,), F32),
            pltpu.SMEM((CH,), F32),
            pltpu.SMEM((CH,), F32),
            pltpu.VMEM((height + 2 * EDGE, width + 2 * LANES), BF16),
            pltpu.VMEM((3, height + 2 * EDGE, width + LANES), BF16),
            pltpu.VMEM((height + 16, 3 * CH, width), BF16),
            pltpu.VMEM((height, width), BF16),
            pltpu.VMEM((16 * CH, 256), BF16),
            pltpu.VMEM((ROWS_OUT * CH, 512), BF16),
            pltpu.SemaphoreType.DMA((8,)),
            pltpu.SemaphoreType.DMA((8,)),
            pltpu.SemaphoreType.DMA((chunks,)),
            pltpu.SemaphoreType.DMA((chunks,)),
            pltpu.SemaphoreType.DMA((7,)),
            pltpu.VMEM((2, height, width), F32),
            pltpu.SemaphoreType.DMA((bands,)),
        ],
        compiler_params=pltpu.CompilerParams(
            collective_id=0, has_side_effects=True, vmem_limit_bytes=64 * 1024 * 1024
        ),
        name="restore_spectra",
    )(section[0], first_kernel, second_kernel, table, first_bias, second_bias, head_weight)
    return pl.pallas_call(
        functools.partial(cross_body, sizes[0]),
        out_shape=jax.ShapeDtypeStruct((1, 2, height, width), F32),
        in_specs=[hbm] * 3,
        out_specs=hbm,
        scratch_shapes=[
            pltpu.VMEM((2, height, width), F32),
            pltpu.VMEM((height, width), BF16),
            pltpu.VMEM((PATCH, 2 * PATCH), F32),
            pltpu.VMEM((2, height, width), F32),
            pltpu.SemaphoreType.DMA((1 + 2 * bands,)),
            pltpu.SemaphoreType.DMA((bands,)),
        ],
        compiler_params=pltpu.CompilerParams(vmem_limit_bytes=64 * 1024 * 1024),
        name="cross_spectra",
    )(spec, following, table)


def solution(mesh):
    sizes = tuple(mesh.shape[name] for name in ("gz", "gy", "gx"))
    placed = (P("gz", "gy", "gx"), P(), P(), P(), P(), P())
    return jax.shard_map(
        functools.partial(on_device, sizes),
        mesh=mesh,
        in_specs=placed,
        out_specs=P("gz", None, "gy", "gx"),
        check_vma=False,
    )
```

```python
import functools
import math

import jax
import jax.numpy as jnp
import numpy as np
from jax import lax
from jax.experimental import pallas as pl
from jax.experimental.pallas import tpu as pltpu
from jax.sharding import PartitionSpec as P

PATCH = 128
CH = 16
EDGE = 16
LANES = 128
ROWS_OUT = 8
F32 = jnp.float32
BF16 = jnp.bfloat16
MESH = pl.DeviceIdType.MESH
SHIFT = jnp.bfloat16
STEPS = [(-1, 0), (1, 0), (0, -1), (0, 1), (-1, -1), (-1, 1), (1, -1), (1, 1)]


def dft_table():
    positions = np.arange(PATCH)
    phase = (positions[:, None] * positions[None, :]) % PATCH
    angles = phase * (2.0 * math.pi / PATCH)
    both = np.concatenate([np.cos(angles), np.sin(angles)], axis=1) / math.sqrt(PATCH)
    return both.astype(np.float32)


def iota(shape, dim):
    return lax.broadcasted_iota(jnp.int32, shape, dim)


def dot(a, b):
    return jnp.dot(a, b, preferred_element_type=F32)


def pieces(value, count):
    out = []
    for _ in range(count):
        part = value.astype(BF16)
        out.append(part)
        value = value - part.astype(F32)
    return out


def column_of(ref):
    ids = iota((CH, 1), 0)
    column = jnp.zeros((CH, 1), F32)
    for c in range(CH):
        column = jnp.where(ids == c, ref[c], column)
    return column


def one_hot(hit):
    return jnp.where(hit, 1.0, 0.0).astype(BF16)


def with_bias(values, ref, lanes, first):
    for n, part in enumerate(pieces(column_of(ref), 3)):
        values = jnp.where(lanes == first + n, part.astype(F32), values)
    return values


def first_weights(kernel_ref, bias_ref):
    rows, depth = 16 * CH, 256
    high, low = pieces(kernel_ref[...], 2)
    k = iota((9, depth), 1)
    tap = iota((9, depth), 0)
    col_off = (k & 127) >> 5
    lanes = iota((CH, depth), 1)
    m = iota((rows, depth), 0)
    kk = iota((rows, depth), 1)
    spread = one_hot((iota((rows, CH), 0) & (CH - 1)) == iota((rows, CH), 1))
    fixed = (kk & 127) >= 96
    offset = (kk & 31) - 14 - (m >> 4)
    weights = jnp.zeros((rows, depth), F32)
    for a in range(3):
        hit = (tap == 3 * a + col_off) & (col_off < 3)
        placed = dot(high, one_hot(hit & (k < 128))) + dot(low, one_hot(hit & (k >= 128)))
        placed = with_bias(placed, bias_ref, lanes, 96)
        weights = jnp.where(fixed | (offset == a), dot(spread, placed.astype(BF16)), weights)
    return weights.astype(BF16)


def second_weights(kernel_ref, bias_ref):
    rows, depth = ROWS_OUT * CH, 512
    flat = kernel_ref[...].reshape(9 * CH, CH)
    tiled = dot(flat, one_hot((iota((CH, depth), 1) & (CH - 1)) == iota((CH, depth), 0)))
    tap = iota((CH, depth), 1) >> 4
    base = jnp.zeros((CH, depth), F32)
    for t in range(9):
        base = jnp.where(tap == t, tiled[t * CH : (t + 1) * CH], base)
    bias = with_bias(jnp.zeros((CH, depth), F32), bias_ref, iota((CH, depth), 1), 480)
    shifted = [base + bias]
    for r in range(1, ROWS_OUT):
        shifted.append(pltpu.roll(base, 3 * CH * r, 1) + bias)
    by_row = jnp.concatenate(shifted, axis=0).astype(BF16)
    m, n = iota((rows, rows), 0), iota((rows, rows), 1)
    order = one_hot(n == (m & (ROWS_OUT - 1)) * CH + (m >> 3))
    return dot(order, by_row).astype(BF16)


def spectrum(image, table):
    cosine, sine = table[:, :PATCH], table[:, PATCH:]
    patches = image.shape[1] // PATCH
    stacked = jnp.concatenate([image[:, n * PATCH : (n + 1) * PATCH] for n in range(patches)], axis=0)
    rows = dot(stacked, table).astype(BF16)
    parts = [rows[n * PATCH : (n + 1) * PATCH] for n in range(patches)]
    lower = jnp.concatenate(
        [
            jnp.concatenate([p[:, :PATCH] for p in parts], axis=1),
            jnp.concatenate([p[:, PATCH:] for p in parts], axis=1),
        ],
        axis=0,
    )
    full = jnp.concatenate(
        [jnp.concatenate([cosine, -sine], axis=1), jnp.concatenate([-sine, -cosine], axis=1)], axis=0
    )
    both = dot(full, lower)
    return both[:PATCH], both[PATCH:]


def chunk_bounds(height):
    return list(range(0, height - PATCH + 1, PATCH)) + [height - PATCH // 2, height - PATCH // 4, height]


def body(
    sizes,
    x_hbm, k1_hbm, k2_hbm, table_hbm, b1_hbm, b2_hbm, hw_hbm,
    out_hbm,
    x_ref, k1_ref, k2_ref, table_ref, b1_ref, b2_ref, hw_ref,
    halo, shifted, hidden, own, following, w1_ref, w2_ref,
    halo_send, halo_recv, next_send, next_recv, local_sem, spec_ref, out_ref, out_sem,
):
    n_gz, n_gy, n_gx = sizes
    height, width = x_ref.shape
    wide = width + LANES
    near = [k1_ref, b1_ref, k2_ref, b2_ref, x_ref, hw_ref, table_ref]
    far = [k1_hbm, b1_hbm, k2_hbm, b2_hbm, x_hbm, hw_hbm, table_hbm]
    loads = [
        pltpu.make_async_copy(source, target, local_sem.at[n])
        for n, (source, target) in enumerate(zip(far, near))
    ]
    for load in loads:
        load.start()
    gz, gy, gx = lax.axis_index("gz"), lax.axis_index("gy"), lax.axis_index("gx")

    def present(dy, dx):
        y, x = gy + dy, gx + dx
        return (y >= 0) & (y < n_gy) & (x >= 0) & (x < n_gx)

    def device(dz, dy, dx):
        return (
            lax.rem(gz + dz + n_gz, n_gz),
            lax.rem(gy + dy + n_gy, n_gy),
            lax.rem(gx + dx + n_gx, n_gx),
        )

    not_first, not_last = gz > 0, gz < n_gz - 1

    barrier = pltpu.get_barrier_semaphore()
    count = not_first.astype(jnp.int32) + not_last.astype(jnp.int32)
    for dy, dx in STEPS:
        count = count + present(dy, dx).astype(jnp.int32)

        @pl.when(present(dy, dx))
        def _():
            pl.semaphore_signal(barrier, inc=1, device_id=device(0, dy, dx), device_id_type=MESH)

    @pl.when(not_first)
    def _():
        pl.semaphore_signal(barrier, inc=1, device_id=device(-1, 0, 0), device_id_type=MESH)

    @pl.when(not_last)
    def _():
        pl.semaphore_signal(barrier, inc=1, device_id=device(1, 0, 0), device_id_type=MESH)

    pl.semaphore_wait(barrier, count)

    row_src = {-1: (0, EDGE), 1: (height - EDGE, EDGE), 0: (0, height)}
    col_src = {-1: (0, LANES), 1: (width - LANES, LANES), 0: (0, width)}
    row_dst = {-1: EDGE + height, 1: 0, 0: EDGE}
    col_dst = {-1: width, 1: width + LANES, 0: 0}
    copies = []
    for n, (dy, dx) in enumerate(STEPS):
        (r0, rn), (c0, cn) = row_src[dy], col_src[dx]
        copies.append(
            pltpu.make_async_remote_copy(
                src_ref=x_hbm.at[pl.ds(r0, rn), pl.ds(c0, cn)],
                dst_ref=halo.at[pl.ds(row_dst[dy], rn), pl.ds(col_dst[dx], cn)],
                send_sem=halo_send.at[n],
                recv_sem=halo_recv.at[n],
                device_id=device(0, dy, dx),
                device_id_type=MESH,
            )
        )
    for n, (dy, dx) in enumerate(STEPS):

        @pl.when(present(dy, dx))
        def _():
            copies[n].start()

        @pl.when(jnp.logical_not(present(-dy, -dx)))
        def _():
            rn, cn = row_src[dy][1], col_src[dx][1]
            halo[pl.ds(row_dst[dy], rn), pl.ds(col_dst[dx], cn)] = jnp.zeros((rn, cn), BF16)

    loads[0].wait()
    loads[1].wait()
    w1_ref[...] = first_weights(k1_ref, b1_ref)
    loads[2].wait()
    loads[3].wait()
    w2_ref[...] = second_weights(k2_ref, b2_ref)
    for load in loads[4:]:
        load.wait()

    def receive(chosen):
        for n in chosen:
            dy, dx = STEPS[n]

            @pl.when(present(-dy, -dx))
            def _():
                copies[n].wait_recv()

    def shift(blocks, step, before, after):
        lane = iota(blocks[0].shape, 1)
        rolled = [pltpu.roll(block, step % LANES, 1) for block in blocks]
        if step > 0:
            fill = [before] + rolled[:-1]
            return [jnp.where(lane == 0, f, r) for f, r in zip(fill, rolled)]
        fill = rolled[1:] + [after]
        return [jnp.where(lane == LANES - 1, f, r) for f, r in zip(fill, rolled)]

    def place(row, size, centre):
        lane = iota((size, LANES), 1)
        right = halo[row : row + size, width : width + LANES]
        left = halo[row : row + size, width + LANES : width + 2 * LANES]
        blocks = [centre[:, n : n + LANES] for n in range(0, width, LANES)]
        left_1, right_1 = pltpu.roll(left, 1, 1), pltpu.roll(right, LANES - 1, 1)
        taps = [
            shift(blocks, 1, left_1, None)
            + [jnp.where(lane == LANES - 1, blocks[-1], pltpu.roll(left, 2, 1))],
            blocks + [jnp.where(lane == LANES - 1, right_1, left_1)],
            shift(blocks, -1, None, right_1)
            + [jnp.where(lane == LANES - 1, pltpu.roll(right, LANES - 2, 1), blocks[0])],
        ]
        for b in range(3):
            shifted[b, row : row + size, :] = jnp.concatenate(taps[b], axis=1)

    def place_edges():
        place(0, EDGE, halo[0:EDGE, 0:width])
        place(EDGE + height, EDGE, halo[EDGE + height : 2 * EDGE + height, 0:width])

    receive((2, 3))
    for row in range(0, height, 64):
        place(EDGE + row, 64, x_ref[row : row + 64, :])

    lane = iota((1, LANES), 1)
    keep = ((lane == 0) & (gx > 0)) | ((lane == LANES - 1) & (gx < n_gx - 1))
    keep = jnp.where(keep, 1.0, 0.0)
    above = jnp.where(gy > 0, 1.0, 0.0)
    below = jnp.where(gy < n_gy - 1, 1.0, 0.0)
    blocks_16 = height // 16

    def first_input(i):
        start = i * 16
        taps = [shifted[b, start : start + 32, :] for b in range(3)]
        return jnp.concatenate(taps + [jnp.ones((32, wide), BF16)] + taps, axis=0)

    def first_output(i, rows, value, outer):
        start = i * 16
        value, outer = jnp.maximum(value, 0.0), jnp.maximum(outer, 0.0) * keep
        if i == 0:
            value = jnp.concatenate([value[:CH] * above, value[CH:]], axis=0)
            outer = jnp.concatenate([outer[:CH] * above, outer[CH:]], axis=0)
        if i == blocks_16:
            value = jnp.concatenate([value[:CH], value[CH : 2 * CH] * below], axis=0)
            outer = jnp.concatenate([outer[:CH], outer[CH : 2 * CH] * below], axis=0)
        outer = outer.astype(SHIFT)
        blocks = [value[:, n : n + LANES].astype(SHIFT) for n in range(0, width, LANES)]
        for b, part in enumerate([shift(blocks, 1, outer, None), blocks, shift(blocks, -1, None, outer)]):
            hidden[start : start + rows, b * CH : (b + 1) * CH, :] = (
                jnp.concatenate(part, axis=1).reshape(rows, CH, width)
            )

    def layer_one(i, rows):
        value = dot(w1_ref[0 : rows * CH, 0:224], first_input(i))
        first_output(i, rows, value[:, :width], value[:, width:])

    def layer_one_pair(i, j):
        one, two = first_input(i), first_input(j)
        weights = w1_ref[:, 0:224]
        outer = dot(weights, jnp.concatenate([one[:, width:], two[:, width:]], axis=1))
        first_output(i, 16, dot(weights, one[:, :width]), outer[:, :LANES])
        first_output(j, 16, dot(weights, two[:, :width]), outer[:, LANES:])

    def layer_two(i):
        start = i * 16
        rows = []
        for g in range(2):
            first = start + g * ROWS_OUT
            window = hidden[first : first + ROWS_OUT + 2, :, :].reshape(480, width)
            stack = jnp.concatenate([window, jnp.ones((16, width), BF16)], axis=0)
            deep = jnp.maximum(dot(w2_ref[:, 0:496], stack), 0.0)
            total = hw_ref[0] * deep[0:ROWS_OUT]
            for o in range(1, CH):
                total = total + hw_ref[o] * deep[o * ROWS_OUT : (o + 1) * ROWS_OUT]
            rows.append(total)
        total = jnp.concatenate(rows, axis=0)
        own[start : start + 16, :] = (x_ref[start : start + 16, :].astype(F32) + total).astype(BF16)

    bands = height // PATCH
    bounds = chunk_bounds(height)
    sends = []
    for n in range(len(bounds) - 1):
        rows = pl.ds(bounds[n], bounds[n + 1] - bounds[n])
        sends.append(
            pltpu.make_async_remote_copy(
                src_ref=own.at[rows, :],
                dst_ref=following.at[rows, :],
                send_sem=next_send.at[n],
                recv_sem=next_recv.at[n],
                device_id=device(-1, 0, 0),
                device_id_type=MESH,
            )
        )

    outs = [
        pltpu.make_async_copy(
            out_ref.at[:, pl.ds(band * PATCH, PATCH), :],
            out_hbm.at[0, :, pl.ds(band * PATCH, PATCH), :],
            out_sem.at[band],
        )
        for band in range(bands)
    ]
    table = table_ref[...].astype(BF16)

    layer_one_pair(1, 2)
    layer_one_pair(3, 4)
    receive((0, 1, 4, 5, 6, 7))
    place_edges()
    layer_one_pair(0, blocks_16 - 1)
    for i in range(blocks_16):
        if i % 2 == 0 and i + 6 < blocks_16 - 1:
            layer_one_pair(i + 5, i + 6)
        elif i + 6 == blocks_16 - 1:
            layer_one(blocks_16, 2)
        layer_two(i)
        if (i + 1) * 16 in bounds:

            @pl.when(not_first)
            def _():
                sends[bounds.index((i + 1) * 16) - 1].start()

        if (i + 1) * 16 % PATCH == 0:
            band = i * 16 // PATCH
            rows = slice(band * PATCH, (band + 1) * PATCH)
            spec_ref[0, rows, :], spec_ref[1, rows, :] = spectrum(own[rows, :], table)

    @pl.when(not_last)
    def _():
        for band in range(bands):
            for n in range(len(sends)):
                if band * PATCH < bounds[n + 1] <= (band + 1) * PATCH:
                    sends[n].wait_recv()
            rows = slice(band * PATCH, (band + 1) * PATCH)
            other_real, other_imag = spectrum(following[rows, :], table)
            real, imag = spec_ref[0, rows, :], spec_ref[1, rows, :]
            out_ref[0, rows, :] = real * other_real + imag * other_imag
            out_ref[1, rows, :] = imag * other_real - real * other_imag
            outs[band].start()

    @pl.when(jnp.logical_not(not_last))
    def _():
        out_ref[...] = jnp.zeros(out_ref.shape, F32)
        for out in outs:
            out.start()

    for n, (dy, dx) in enumerate(STEPS):

        @pl.when(present(dy, dx))
        def _():
            copies[n].wait_send()

    @pl.when(not_first)
    def _():
        for send in sends:
            send.wait_send()

    for out in outs:
        out.wait()


def copy_body(source, target, sems):
    height = source.shape[2]
    part = height // 2
    copies = []
    for n in range(4):
        place = (0, n // 2, pl.ds((n % 2) * part, part), slice(None))
        copies.append(pltpu.make_async_copy(source.at[place], target.at[place], sems.at[n]))
    for copy in copies:
        copy.start()
    for copy in copies:
        copy.wait()


def on_device(sizes, section, first_kernel, first_bias, second_kernel, second_bias, head_weight):
    height, width = section.shape[1:]
    bands = height // PATCH
    chunks = len(chunk_bounds(height)) - 1
    hbm = pl.BlockSpec(memory_space=pltpu.HBM)
    table = jnp.asarray(dft_table())
    product = pl.pallas_call(
        functools.partial(body, sizes),
        out_shape=jax.ShapeDtypeStruct((1, 2, height, width), F32),
        in_specs=[hbm] * 7,
        out_specs=hbm,
        scratch_shapes=[
            pltpu.VMEM((height, width), BF16),
            pltpu.VMEM(first_kernel.shape, F32),
            pltpu.VMEM(second_kernel.shape, BF16),
            pltpu.VMEM((PATCH, 2 * PATCH), F32),
            pltpu.SMEM((CH,), F32),
            pltpu.SMEM((CH,), F32),
            pltpu.SMEM((CH,), F32),
            pltpu.VMEM((height + 2 * EDGE, width + 2 * LANES), BF16),
            pltpu.VMEM((3, height + 2 * EDGE, width + LANES), BF16),
            pltpu.VMEM((height + 16, 3 * CH, width), BF16),
            pltpu.VMEM((height, width), BF16),
            pltpu.VMEM((height, width), BF16),
            pltpu.VMEM((16 * CH, 256), BF16),
            pltpu.VMEM((ROWS_OUT * CH, 512), BF16),
            pltpu.SemaphoreType.DMA((8,)),
            pltpu.SemaphoreType.DMA((8,)),
            pltpu.SemaphoreType.DMA((chunks,)),
            pltpu.SemaphoreType.DMA((chunks,)),
            pltpu.SemaphoreType.DMA((7,)),
            pltpu.VMEM((2, height, width), F32),
            pltpu.VMEM((2, height, width), F32),
            pltpu.SemaphoreType.DMA((bands,)),
        ],
        compiler_params=pltpu.CompilerParams(
            collective_id=0, has_side_effects=True, vmem_limit_bytes=64 * 1024 * 1024
        ),
        name="restore_spectra",
    )(section[0], first_kernel, second_kernel, table, first_bias, second_bias, head_weight)
    return pl.pallas_call(
        copy_body,
        out_shape=jax.ShapeDtypeStruct(product.shape, F32),
        in_specs=[hbm],
        out_specs=hbm,
        scratch_shapes=[pltpu.SemaphoreType.DMA((4,))],
        compiler_params=pltpu.CompilerParams(vmem_limit_bytes=64 * 1024 * 1024),
        name="write_result",
    )(product)


def solution(mesh):
    sizes = tuple(mesh.shape[name] for name in ("gz", "gy", "gx"))
    placed = (P("gz", "gy", "gx"), P(), P(), P(), P(), P())
    return jax.shard_map(
        functools.partial(on_device, sizes),
        mesh=mesh,
        in_specs=placed,
        out_specs=P("gz", None, "gy", "gx"),
        check_vma=False,
    )
```

```python
import functools
import math

import jax
import jax.numpy as jnp
import numpy as np
from jax import lax
from jax.experimental import pallas as pl
from jax.experimental.pallas import tpu as pltpu
from jax.sharding import PartitionSpec as P

PATCH = 128
CH = 16
EDGE = 16
LANES = 128
ROWS_OUT = 8
F32 = jnp.float32
BF16 = jnp.bfloat16
MESH = pl.DeviceIdType.MESH
SHIFT = jnp.bfloat16
STEPS = [(-1, 0), (1, 0), (0, -1), (0, 1), (-1, -1), (-1, 1), (1, -1), (1, 1)]


def dft_table():
    positions = np.arange(PATCH)
    phase = (positions[:, None] * positions[None, :]) % PATCH
    angles = phase * (2.0 * math.pi / PATCH)
    both = np.concatenate([np.cos(angles), np.sin(angles)], axis=1) / math.sqrt(PATCH)
    return both.astype(np.float32)


def iota(shape, dim):
    return lax.broadcasted_iota(jnp.int32, shape, dim)


def dot(a, b):
    return jnp.dot(a, b, preferred_element_type=F32)


def pieces(value, count):
    out = []
    for _ in range(count):
        part = value.astype(BF16)
        out.append(part)
        value = value - part.astype(F32)
    return out


def column_of(ref):
    ids = iota((CH, 1), 0)
    column = jnp.zeros((CH, 1), F32)
    for c in range(CH):
        column = jnp.where(ids == c, ref[c], column)
    return column


def one_hot(hit):
    return jnp.where(hit, 1.0, 0.0).astype(BF16)


def with_bias(values, ref, lanes, first):
    for n, part in enumerate(pieces(column_of(ref), 3)):
        values = jnp.where(lanes == first + n, part.astype(F32), values)
    return values


def first_weights(kernel_ref, bias_ref):
    rows, depth = 16 * CH, 256
    high, low = pieces(kernel_ref[...], 2)
    k = iota((9, depth), 1)
    tap = iota((9, depth), 0)
    col_off = (k & 127) >> 5
    lanes = iota((CH, depth), 1)
    m = iota((rows, depth), 0)
    kk = iota((rows, depth), 1)
    spread = one_hot((iota((rows, CH), 0) & (CH - 1)) == iota((rows, CH), 1))
    fixed = (kk & 127) >= 96
    offset = (kk & 31) - 14 - (m >> 4)
    weights = jnp.zeros((rows, depth), F32)
    for a in range(3):
        hit = (tap == 3 * a + col_off) & (col_off < 3)
        placed = dot(high, one_hot(hit & (k < 128))) + dot(low, one_hot(hit & (k >= 128)))
        placed = with_bias(placed, bias_ref, lanes, 96)
        weights = jnp.where(fixed | (offset == a), dot(spread, placed.astype(BF16)), weights)
    return weights.astype(BF16)


def second_weights(kernel_ref, bias_ref):
    rows, depth = ROWS_OUT * CH, 512
    flat = kernel_ref[...].reshape(9 * CH, CH)
    tiled = dot(flat, one_hot((iota((CH, depth), 1) & (CH - 1)) == iota((CH, depth), 0)))
    tap = iota((CH, depth), 1) >> 4
    base = jnp.zeros((CH, depth), F32)
    for t in range(9):
        base = jnp.where(tap == t, tiled[t * CH : (t + 1) * CH], base)
    bias = with_bias(jnp.zeros((CH, depth), F32), bias_ref, iota((CH, depth), 1), 480)
    shifted = [base + bias]
    for r in range(1, ROWS_OUT):
        shifted.append(pltpu.roll(base, 3 * CH * r, 1) + bias)
    by_row = jnp.concatenate(shifted, axis=0).astype(BF16)
    m, n = iota((rows, rows), 0), iota((rows, rows), 1)
    order = one_hot(n == (m & (ROWS_OUT - 1)) * CH + (m >> 3))
    return dot(order, by_row).astype(BF16)


def spectrum(image, table):
    cosine, sine = table[:, :PATCH], table[:, PATCH:]
    patches = image.shape[1] // PATCH
    stacked = jnp.concatenate([image[:, n * PATCH : (n + 1) * PATCH] for n in range(patches)], axis=0)
    rows = dot(stacked, table).astype(BF16)
    parts = [rows[n * PATCH : (n + 1) * PATCH] for n in range(patches)]
    lower = jnp.concatenate(
        [
            jnp.concatenate([p[:, :PATCH] for p in parts], axis=1),
            jnp.concatenate([p[:, PATCH:] for p in parts], axis=1),
        ],
        axis=0,
    )
    full = jnp.concatenate(
        [jnp.concatenate([cosine, -sine], axis=1), jnp.concatenate([-sine, -cosine], axis=1)], axis=0
    )
    both = dot(full, lower)
    return both[:PATCH], both[PATCH:]


def chunk_bounds(height):
    return list(range(0, height - 31, 32)) + [height - 16, height]


def body(
    sizes,
    x_hbm, k1_hbm, k2_hbm, table_hbm, b1_hbm, b2_hbm, hw_hbm,
    product_hbm, spec_hbm, tail_hbm,
    x_ref, k1_ref, k2_ref, table_ref, b1_ref, b2_ref, hw_ref,
    halo, shifted, hidden, own, following, w1_ref, w2_ref,
    halo_send, halo_recv, next_send, next_recv, local_sem, spec_ref, product_ref, out_sem,
):
    n_gz, n_gy, n_gx = sizes
    height, width = x_ref.shape
    wide = width + LANES
    near = [k1_ref, b1_ref, k2_ref, b2_ref, x_ref, hw_ref, table_ref]
    far = [k1_hbm, b1_hbm, k2_hbm, b2_hbm, x_hbm, hw_hbm, table_hbm]
    loads = [
        pltpu.make_async_copy(source, target, local_sem.at[n])
        for n, (source, target) in enumerate(zip(far, near))
    ]
    for load in loads:
        load.start()
    gz, gy, gx = lax.axis_index("gz"), lax.axis_index("gy"), lax.axis_index("gx")

    def present(dy, dx):
        y, x = gy + dy, gx + dx
        return (y >= 0) & (y < n_gy) & (x >= 0) & (x < n_gx)

    def device(dz, dy, dx):
        return (
            lax.rem(gz + dz + n_gz, n_gz),
            lax.rem(gy + dy + n_gy, n_gy),
            lax.rem(gx + dx + n_gx, n_gx),
        )

    barrier = pltpu.get_barrier_semaphore()
    count = jnp.int32(2)
    for dy, dx in STEPS:
        count = count + present(dy, dx).astype(jnp.int32)

        @pl.when(present(dy, dx))
        def _():
            pl.semaphore_signal(barrier, inc=1, device_id=device(0, dy, dx), device_id_type=MESH)

    for dz in (-1, 1):
        pl.semaphore_signal(barrier, inc=1, device_id=device(dz, 0, 0), device_id_type=MESH)

    pl.semaphore_wait(barrier, count)

    row_src = {-1: (0, EDGE), 1: (height - EDGE, EDGE), 0: (0, height)}
    col_src = {-1: (0, LANES), 1: (width - LANES, LANES), 0: (0, width)}
    row_dst = {-1: EDGE + height, 1: 0, 0: EDGE}
    col_dst = {-1: width, 1: width + LANES, 0: 0}
    copies = []
    for n, (dy, dx) in enumerate(STEPS):
        (r0, rn), (c0, cn) = row_src[dy], col_src[dx]
        copies.append(
            pltpu.make_async_remote_copy(
                src_ref=x_hbm.at[pl.ds(r0, rn), pl.ds(c0, cn)],
                dst_ref=halo.at[pl.ds(row_dst[dy], rn), pl.ds(col_dst[dx], cn)],
                send_sem=halo_send.at[n],
                recv_sem=halo_recv.at[n],
                device_id=device(0, dy, dx),
                device_id_type=MESH,
            )
        )
    for n, (dy, dx) in enumerate(STEPS):

        @pl.when(present(dy, dx))
        def _():
            copies[n].start()

        @pl.when(jnp.logical_not(present(-dy, -dx)))
        def _():
            rn, cn = row_src[dy][1], col_src[dx][1]
            halo[pl.ds(row_dst[dy], rn), pl.ds(col_dst[dx], cn)] = jnp.zeros((rn, cn), BF16)

    loads[0].wait()
    loads[1].wait()
    w1_ref[...] = first_weights(k1_ref, b1_ref)
    loads[2].wait()
    loads[3].wait()
    w2_ref[...] = second_weights(k2_ref, b2_ref)
    for load in loads[4:]:
        load.wait()

    def receive(chosen):
        for n in chosen:
            dy, dx = STEPS[n]

            @pl.when(present(-dy, -dx))
            def _():
                copies[n].wait_recv()

    def shift(blocks, step, before, after):
        lane = iota(blocks[0].shape, 1)
        rolled = [pltpu.roll(block, step % LANES, 1) for block in blocks]
        if step > 0:
            fill = [before] + rolled[:-1]
            return [jnp.where(lane == 0, f, r) for f, r in zip(fill, rolled)]
        fill = rolled[1:] + [after]
        return [jnp.where(lane == LANES - 1, f, r) for f, r in zip(fill, rolled)]

    def place(row, size, centre):
        lane = iota((size, LANES), 1)
        right = halo[row : row + size, width : width + LANES]
        left = halo[row : row + size, width + LANES : width + 2 * LANES]
        blocks = [centre[:, n : n + LANES] for n in range(0, width, LANES)]
        left_1, right_1 = pltpu.roll(left, 1, 1), pltpu.roll(right, LANES - 1, 1)
        taps = [
            shift(blocks, 1, left_1, None)
            + [jnp.where(lane == LANES - 1, blocks[-1], pltpu.roll(left, 2, 1))],
            blocks + [jnp.where(lane == LANES - 1, right_1, left_1)],
            shift(blocks, -1, None, right_1)
            + [jnp.where(lane == LANES - 1, pltpu.roll(right, LANES - 2, 1), blocks[0])],
        ]
        for b in range(3):
            shifted[b, row : row + size, :] = jnp.concatenate(taps[b], axis=1)

    def place_edges():
        place(0, EDGE, halo[0:EDGE, 0:width])
        place(EDGE + height, EDGE, halo[EDGE + height : 2 * EDGE + height, 0:width])

    receive((2, 3))
    for row in range(0, height, 64):
        place(EDGE + row, 64, x_ref[row : row + 64, :])

    lane = iota((1, LANES), 1)
    keep = ((lane == 0) & (gx > 0)) | ((lane == LANES - 1) & (gx < n_gx - 1))
    keep = jnp.where(keep, 1.0, 0.0)
    above = jnp.where(gy > 0, 1.0, 0.0)
    below = jnp.where(gy < n_gy - 1, 1.0, 0.0)
    blocks_16 = height // 16

    def first_input(i):
        start = i * 16
        taps = [shifted[b, start : start + 32, :] for b in range(3)]
        return jnp.concatenate(taps + [jnp.ones((32, wide), BF16)] + taps, axis=0)

    def first_output(i, rows, value, outer):
        start = i * 16
        value, outer = jnp.maximum(value, 0.0), jnp.maximum(outer, 0.0) * keep
        if i == 0:
            value = jnp.concatenate([value[:CH] * above, value[CH:]], axis=0)
            outer = jnp.concatenate([outer[:CH] * above, outer[CH:]], axis=0)
        if i == blocks_16:
            value = jnp.concatenate([value[:CH], value[CH : 2 * CH] * below], axis=0)
            outer = jnp.concatenate([outer[:CH], outer[CH : 2 * CH] * below], axis=0)
        outer = outer.astype(SHIFT)
        blocks = [value[:, n : n + LANES].astype(SHIFT) for n in range(0, width, LANES)]
        for b, part in enumerate([shift(blocks, 1, outer, None), blocks, shift(blocks, -1, None, outer)]):
            hidden[start : start + rows, b * CH : (b + 1) * CH, :] = (
                jnp.concatenate(part, axis=1).reshape(rows, CH, width)
            )

    def layer_one(i, rows):
        value = dot(w1_ref[0 : rows * CH, 0:224], first_input(i))
        first_output(i, rows, value[:, :width], value[:, width:])

    def layer_one_pair(i, j):
        one, two = first_input(i), first_input(j)
        weights = w1_ref[:, 0:224]
        outer = dot(weights, jnp.concatenate([one[:, width:], two[:, width:]], axis=1))
        first_output(i, 16, dot(weights, one[:, :width]), outer[:, :LANES])
        first_output(j, 16, dot(weights, two[:, :width]), outer[:, LANES:])

    def layer_two(i):
        start = i * 16
        rows = []
        for g in range(2):
            first = start + g * ROWS_OUT
            window = hidden[first : first + ROWS_OUT + 2, :, :].reshape(480, width)
            stack = jnp.concatenate([window, jnp.ones((16, width), BF16)], axis=0)
            deep = jnp.maximum(dot(w2_ref[:, 0:496], stack), 0.0)
            total = hw_ref[0] * deep[0:ROWS_OUT]
            for o in range(1, CH):
                total = total + hw_ref[o] * deep[o * ROWS_OUT : (o + 1) * ROWS_OUT]
            rows.append(total)
        total = jnp.concatenate(rows, axis=0)
        own[start : start + 16, :] = (x_ref[start : start + 16, :].astype(F32) + total).astype(BF16)

    bands = height // PATCH
    bounds = chunk_bounds(height)
    sends = []
    for n in range(len(bounds) - 1):
        rows = pl.ds(bounds[n], bounds[n + 1] - bounds[n])
        if bounds[n + 1] <= height - PATCH:
            target = following.at[rows, :]
        else:
            target = tail_hbm.at[pl.ds(bounds[n] - height + PATCH, bounds[n + 1] - bounds[n]), :]
        sends.append(
            pltpu.make_async_remote_copy(
                src_ref=own.at[rows, :],
                dst_ref=target,
                send_sem=next_send.at[n],
                recv_sem=next_recv.at[n],
                device_id=device(-1, 0, 0),
                device_id_type=MESH,
            )
        )

    early = height - PATCH
    outs = [
        pltpu.make_async_copy(product_ref, product_hbm, out_sem.at[0]),
        pltpu.make_async_copy(spec_ref.at[:, pl.ds(early, PATCH), :], spec_hbm, out_sem.at[1]),
    ]
    table = table_ref[...].astype(BF16)

    layer_one_pair(1, 2)
    layer_one_pair(3, 4)
    receive((0, 1, 4, 5, 6, 7))
    place_edges()
    layer_one_pair(0, blocks_16 - 1)
    for i in range(blocks_16):
        if i % 2 == 0 and i + 6 < blocks_16 - 1:
            layer_one_pair(i + 5, i + 6)
        elif i + 6 == blocks_16 - 1:
            layer_one(blocks_16, 2)
        layer_two(i)
        if (i + 1) * 16 in bounds:
            sends[bounds.index((i + 1) * 16) - 1].start()
        if (i + 1) * 16 % PATCH == 0:
            band = i * 16 // PATCH
            rows = slice(band * PATCH, (band + 1) * PATCH)
            spec_ref[0, rows, :], spec_ref[1, rows, :] = spectrum(own[rows, :], table)

    outs[1].start()
    for n in range(len(sends)):
        if bounds[n + 1] <= early:
            sends[n].wait_recv()
    for band in range(bands - 1):
        rows = slice(band * PATCH, (band + 1) * PATCH)
        other_real, other_imag = spectrum(following[rows, :], table)
        real, imag = spec_ref[0, rows, :], spec_ref[1, rows, :]
        product_ref[0, rows, :] = real * other_real + imag * other_imag
        product_ref[1, rows, :] = imag * other_real - real * other_imag
    outs[0].start()

    for n, (dy, dx) in enumerate(STEPS):

        @pl.when(present(dy, dx))
        def _():
            copies[n].wait_send()

    for n in range(len(sends)):
        sends[n].wait_send()
        if bounds[n + 1] > early:
            sends[n].wait_recv()
    for out in outs:
        out.wait()


def cross_body(
    n_gz,
    product_hbm, spec_hbm, tail_hbm, table_hbm,
    out_hbm,
    spec, tail, table_ref, out_ref, sems, out_sems,
):
    early = out_ref.shape[1] - PATCH
    not_last = lax.axis_index("gz") < n_gz - 1
    outs = [
        pltpu.make_async_copy(
            out_ref.at[:, pl.ds(start, size), :], out_hbm.at[0, :, pl.ds(start, size), :], out_sems.at[n]
        )
        for n, (start, size) in enumerate([(0, early), (early, PATCH)])
    ]

    @pl.when(not_last)
    def _():
        targets = [table_ref, tail, spec, out_ref.at[:, pl.ds(0, early), :]]
        sources = [table_hbm, tail_hbm, spec_hbm, product_hbm]
        loads = [
            pltpu.make_async_copy(source, target, sems.at[n])
            for n, (source, target) in enumerate(zip(sources, targets))
        ]
        for load in loads:
            load.start()
        loads[0].wait()
        table = table_ref[...].astype(BF16)
        loads[1].wait()
        other_real, other_imag = spectrum(tail[...], table)
        loads[2].wait()
        real, imag = spec[0], spec[1]
        out_ref[0, early:, :] = real * other_real + imag * other_imag
        out_ref[1, early:, :] = imag * other_real - real * other_imag
        outs[1].start()
        loads[3].wait()
        outs[0].start()

    @pl.when(jnp.logical_not(not_last))
    def _():
        out_ref[...] = jnp.zeros(out_ref.shape, F32)
        for out in outs:
            out.start()

    for out in outs:
        out.wait()


def on_device(sizes, section, first_kernel, first_bias, second_kernel, second_bias, head_weight):
    height, width = section.shape[1:]
    chunks = len(chunk_bounds(height)) - 1
    hbm = pl.BlockSpec(memory_space=pltpu.HBM)
    table = jnp.asarray(dft_table())
    early = height - PATCH
    product, spec, tail = pl.pallas_call(
        functools.partial(body, sizes),
        out_shape=[
            jax.ShapeDtypeStruct((2, early, width), F32),
            jax.ShapeDtypeStruct((2, PATCH, width), F32),
            jax.ShapeDtypeStruct((PATCH, width), BF16),
        ],
        in_specs=[hbm] * 7,
        out_specs=[hbm] * 3,
        scratch_shapes=[
            pltpu.VMEM((height, width), BF16),
            pltpu.VMEM(first_kernel.shape, F32),
            pltpu.VMEM(second_kernel.shape, BF16),
            pltpu.VMEM((PATCH, 2 * PATCH), F32),
            pltpu.SMEM((CH,), F32),
            pltpu.SMEM((CH,), F32),
            pltpu.SMEM((CH,), F32),
            pltpu.VMEM((height + 2 * EDGE, width + 2 * LANES), BF16),
            pltpu.VMEM((3, height + 2 * EDGE, width + LANES), BF16),
            pltpu.VMEM((height + 16, 3 * CH, width), BF16),
            pltpu.VMEM((height, width), BF16),
            pltpu.VMEM((early, width), BF16),
            pltpu.VMEM((16 * CH, 256), BF16),
            pltpu.VMEM((ROWS_OUT * CH, 512), BF16),
            pltpu.SemaphoreType.DMA((8,)),
            pltpu.SemaphoreType.DMA((8,)),
            pltpu.SemaphoreType.DMA((chunks,)),
            pltpu.SemaphoreType.DMA((chunks,)),
            pltpu.SemaphoreType.DMA((7,)),
            pltpu.VMEM((2, height, width), F32),
            pltpu.VMEM((2, early, width), F32),
            pltpu.SemaphoreType.DMA((2,)),
        ],
        compiler_params=pltpu.CompilerParams(
            collective_id=0, has_side_effects=True, vmem_limit_bytes=64 * 1024 * 1024
        ),
        name="restore_spectra",
    )(section[0], first_kernel, second_kernel, table, first_bias, second_bias, head_weight)
    return pl.pallas_call(
        functools.partial(cross_body, sizes[0]),
        out_shape=jax.ShapeDtypeStruct((1, 2, height, width), F32),
        in_specs=[hbm] * 4,
        out_specs=hbm,
        scratch_shapes=[
            pltpu.VMEM((2, PATCH, width), F32),
            pltpu.VMEM((PATCH, width), BF16),
            pltpu.VMEM((PATCH, 2 * PATCH), F32),
            pltpu.VMEM((2, height, width), F32),
            pltpu.SemaphoreType.DMA((4,)),
            pltpu.SemaphoreType.DMA((2,)),
        ],
        compiler_params=pltpu.CompilerParams(vmem_limit_bytes=64 * 1024 * 1024),
        name="cross_spectra",
    )(product, spec, tail, table)


def solution(mesh):
    sizes = tuple(mesh.shape[name] for name in ("gz", "gy", "gx"))
    placed = (P("gz", "gy", "gx"), P(), P(), P(), P(), P())
    return jax.shard_map(
        functools.partial(on_device, sizes),
        mesh=mesh,
        in_specs=placed,
        out_specs=P("gz", None, "gy", "gx"),
        check_vma=False,
    )
```

```python
import functools
import math

import jax
import jax.numpy as jnp
import numpy as np
from jax import lax
from jax.experimental import pallas as pl
from jax.experimental.pallas import tpu as pltpu
from jax.sharding import PartitionSpec as P

PATCH = 128
CH = 16
EDGE = 16
LANES = 128
ROWS_OUT = 8
F32 = jnp.float32
BF16 = jnp.bfloat16
MESH = pl.DeviceIdType.MESH
SHIFT = jnp.bfloat16
STEPS = [(-1, 0), (1, 0), (0, -1), (0, 1), (-1, -1), (-1, 1), (1, -1), (1, 1)]


def dft_table():
    positions = np.arange(PATCH)
    phase = (positions[:, None] * positions[None, :]) % PATCH
    angles = phase * (2.0 * math.pi / PATCH)
    both = np.concatenate([np.cos(angles), np.sin(angles)], axis=1) / math.sqrt(PATCH)
    return both.astype(np.float32)


def iota(shape, dim):
    return lax.broadcasted_iota(jnp.int32, shape, dim)


def dot(a, b):
    return jnp.dot(a, b, preferred_element_type=F32)


def pieces(value, count):
    out = []
    for _ in range(count):
        part = value.astype(BF16)
        out.append(part)
        value = value - part.astype(F32)
    return out


def column_of(ref):
    ids = iota((CH, 1), 0)
    column = jnp.zeros((CH, 1), F32)
    for c in range(CH):
        column = jnp.where(ids == c, ref[c], column)
    return column


def one_hot(hit):
    return jnp.where(hit, 1.0, 0.0).astype(BF16)


def with_bias(values, ref, lanes, first):
    for n, part in enumerate(pieces(column_of(ref), 3)):
        values = jnp.where(lanes == first + n, part.astype(F32), values)
    return values


def first_weights(kernel_ref, bias_ref):
    rows, depth = 16 * CH, 256
    high, low = pieces(kernel_ref[...], 2)
    k = iota((9, depth), 1)
    tap = iota((9, depth), 0)
    col_off = (k & 127) >> 5
    lanes = iota((CH, depth), 1)
    m = iota((rows, depth), 0)
    kk = iota((rows, depth), 1)
    spread = one_hot((iota((rows, CH), 0) & (CH - 1)) == iota((rows, CH), 1))
    fixed = (kk & 127) >= 96
    offset = (kk & 31) - 14 - (m >> 4)
    weights = jnp.zeros((rows, depth), F32)
    for a in range(3):
        hit = (tap == 3 * a + col_off) & (col_off < 3)
        placed = dot(high, one_hot(hit & (k < 128))) + dot(low, one_hot(hit & (k >= 128)))
        placed = with_bias(placed, bias_ref, lanes, 96)
        weights = jnp.where(fixed | (offset == a), dot(spread, placed.astype(BF16)), weights)
    return weights.astype(BF16)


def second_weights(kernel_ref, bias_ref):
    rows, depth = ROWS_OUT * CH, 512
    flat = kernel_ref[...].reshape(9 * CH, CH)
    tiled = dot(flat, one_hot((iota((CH, depth), 1) & (CH - 1)) == iota((CH, depth), 0)))
    tap = iota((CH, depth), 1) >> 4
    base = jnp.zeros((CH, depth), F32)
    for t in range(9):
        base = jnp.where(tap == t, tiled[t * CH : (t + 1) * CH], base)
    bias = with_bias(jnp.zeros((CH, depth), F32), bias_ref, iota((CH, depth), 1), 480)
    shifted = [base + bias]
    for r in range(1, ROWS_OUT):
        shifted.append(pltpu.roll(base, 3 * CH * r, 1) + bias)
    by_row = jnp.concatenate(shifted, axis=0).astype(BF16)
    m, n = iota((rows, rows), 0), iota((rows, rows), 1)
    order = one_hot(n == (m & (ROWS_OUT - 1)) * CH + (m >> 3))
    return dot(order, by_row).astype(BF16)


def spectrum(image, table):
    cosine, sine = table[:, :PATCH], table[:, PATCH:]
    patches = image.shape[1] // PATCH
    stacked = jnp.concatenate([image[:, n * PATCH : (n + 1) * PATCH] for n in range(patches)], axis=0)
    rows = dot(stacked, table).astype(BF16)
    parts = [rows[n * PATCH : (n + 1) * PATCH] for n in range(patches)]
    lower = jnp.concatenate(
        [
            jnp.concatenate([p[:, :PATCH] for p in parts], axis=1),
            jnp.concatenate([p[:, PATCH:] for p in parts], axis=1),
        ],
        axis=0,
    )
    full = jnp.concatenate(
        [jnp.concatenate([cosine, -sine], axis=1), jnp.concatenate([-sine, -cosine], axis=1)], axis=0
    )
    both = dot(full, lower)
    return both[:PATCH], both[PATCH:]


def chunk_bounds(height):
    return list(range(0, height - 31, 32)) + [height - 16, height]


def body(
    sizes,
    x_hbm, k1_hbm, k2_hbm, table_hbm, b1_hbm, b2_hbm, hw_hbm,
    product_hbm, spec_hbm, tail_hbm,
    x_ref, k1_ref, k2_ref, table_ref, b1_ref, b2_ref, hw_ref,
    halo, shifted, hidden, own, following, w1_ref, w2_ref,
    halo_send, halo_recv, next_send, next_recv, local_sem, spec_ref, product_ref, out_sem,
):
    n_gz, n_gy, n_gx = sizes
    height, width = x_ref.shape
    wide = width + LANES
    near = [k1_ref, b1_ref, k2_ref, b2_ref, x_ref, hw_ref, table_ref]
    far = [k1_hbm, b1_hbm, k2_hbm, b2_hbm, x_hbm, hw_hbm, table_hbm]
    loads = [
        pltpu.make_async_copy(source, target, local_sem.at[n])
        for n, (source, target) in enumerate(zip(far, near))
    ]
    for load in loads:
        load.start()
    gz, gy, gx = lax.axis_index("gz"), lax.axis_index("gy"), lax.axis_index("gx")

    def present(dy, dx):
        y, x = gy + dy, gx + dx
        return (y >= 0) & (y < n_gy) & (x >= 0) & (x < n_gx)

    def device(dz, dy, dx):
        return (
            lax.rem(gz + dz + n_gz, n_gz),
            lax.rem(gy + dy + n_gy, n_gy),
            lax.rem(gx + dx + n_gx, n_gx),
        )

    barrier = pltpu.get_barrier_semaphore()
    count = jnp.int32(2)
    for dy, dx in STEPS:
        count = count + present(dy, dx).astype(jnp.int32)

        @pl.when(present(dy, dx))
        def _():
            pl.semaphore_signal(barrier, inc=1, device_id=device(0, dy, dx), device_id_type=MESH)

    for dz in (-1, 1):
        pl.semaphore_signal(barrier, inc=1, device_id=device(dz, 0, 0), device_id_type=MESH)

    pl.semaphore_wait(barrier, count)

    row_src = {-1: (0, EDGE), 1: (height - EDGE, EDGE), 0: (0, height)}
    col_src = {-1: (0, LANES), 1: (width - LANES, LANES), 0: (0, width)}
    row_dst = {-1: EDGE + height, 1: 0, 0: EDGE}
    col_dst = {-1: width, 1: width + LANES, 0: 0}
    copies = []
    for n, (dy, dx) in enumerate(STEPS):
        (r0, rn), (c0, cn) = row_src[dy], col_src[dx]
        copies.append(
            pltpu.make_async_remote_copy(
                src_ref=x_hbm.at[pl.ds(r0, rn), pl.ds(c0, cn)],
                dst_ref=halo.at[pl.ds(row_dst[dy], rn), pl.ds(col_dst[dx], cn)],
                send_sem=halo_send.at[n],
                recv_sem=halo_recv.at[n],
                device_id=device(0, dy, dx),
                device_id_type=MESH,
            )
        )
    for n, (dy, dx) in enumerate(STEPS):

        @pl.when(present(dy, dx))
        def _():
            copies[n].start()

        @pl.when(jnp.logical_not(present(-dy, -dx)))
        def _():
            rn, cn = row_src[dy][1], col_src[dx][1]
            halo[pl.ds(row_dst[dy], rn), pl.ds(col_dst[dx], cn)] = jnp.zeros((rn, cn), BF16)

    loads[0].wait()
    loads[1].wait()
    w1_ref[...] = first_weights(k1_ref, b1_ref)
    loads[2].wait()
    loads[3].wait()
    w2_ref[...] = second_weights(k2_ref, b2_ref)
    for load in loads[4:]:
        load.wait()

    def receive(chosen):
        for n in chosen:
            dy, dx = STEPS[n]

            @pl.when(present(-dy, -dx))
            def _():
                copies[n].wait_recv()

    def shift(blocks, step, before, after):
        lane = iota(blocks[0].shape, 1)
        rolled = [pltpu.roll(block, step % LANES, 1) for block in blocks]
        if step > 0:
            fill = [before] + rolled[:-1]
            return [jnp.where(lane == 0, f, r) for f, r in zip(fill, rolled)]
        fill = rolled[1:] + [after]
        return [jnp.where(lane == LANES - 1, f, r) for f, r in zip(fill, rolled)]

    def place(row, size, centre):
        lane = iota((size, LANES), 1)
        right = halo[row : row + size, width : width + LANES]
        left = halo[row : row + size, width + LANES : width + 2 * LANES]
        blocks = [centre[:, n : n + LANES] for n in range(0, width, LANES)]
        left_1, right_1 = pltpu.roll(left, 1, 1), pltpu.roll(right, LANES - 1, 1)
        taps = [
            shift(blocks, 1, left_1, None)
            + [jnp.where(lane == LANES - 1, blocks[-1], pltpu.roll(left, 2, 1))],
            blocks + [jnp.where(lane == LANES - 1, right_1, left_1)],
            shift(blocks, -1, None, right_1)
            + [jnp.where(lane == LANES - 1, pltpu.roll(right, LANES - 2, 1), blocks[0])],
        ]
        for b in range(3):
            shifted[b, row : row + size, :] = jnp.concatenate(taps[b], axis=1)

    def place_edges():
        place(0, EDGE, halo[0:EDGE, 0:width])
        place(EDGE + height, EDGE, halo[EDGE + height : 2 * EDGE + height, 0:width])

    receive((2, 3))
    for row in range(0, height, 64):
        place(EDGE + row, 64, x_ref[row : row + 64, :])

    lane = iota((1, LANES), 1)
    keep = ((lane == 0) & (gx > 0)) | ((lane == LANES - 1) & (gx < n_gx - 1))
    keep = jnp.where(keep, 1.0, 0.0)
    above = jnp.where(gy > 0, 1.0, 0.0)
    below = jnp.where(gy < n_gy - 1, 1.0, 0.0)
    blocks_16 = height // 16

    def first_input(i):
        start = i * 16
        taps = [shifted[b, start : start + 32, :] for b in range(3)]
        return jnp.concatenate(taps + [jnp.ones((32, wide), BF16)] + taps, axis=0)

    def first_output(i, rows, value, outer):
        start = i * 16
        value, outer = jnp.maximum(value, 0.0), jnp.maximum(outer, 0.0) * keep
        if i == 0:
            value = jnp.concatenate([value[:CH] * above, value[CH:]], axis=0)
            outer = jnp.concatenate([outer[:CH] * above, outer[CH:]], axis=0)
        if i == blocks_16:
            value = jnp.concatenate([value[:CH], value[CH : 2 * CH] * below], axis=0)
            outer = jnp.concatenate([outer[:CH], outer[CH : 2 * CH] * below], axis=0)
        outer = outer.astype(SHIFT)
        blocks = [value[:, n : n + LANES].astype(SHIFT) for n in range(0, width, LANES)]
        for b, part in enumerate([shift(blocks, 1, outer, None), blocks, shift(blocks, -1, None, outer)]):
            hidden[start : start + rows, b * CH : (b + 1) * CH, :] = (
                jnp.concatenate(part, axis=1).reshape(rows, CH, width)
            )

    def layer_one(i, rows):
        value = dot(w1_ref[0 : rows * CH, 0:224], first_input(i))
        first_output(i, rows, value[:, :width], value[:, width:])

    def layer_one_pair(i, j):
        one, two = first_input(i), first_input(j)
        stack = jnp.concatenate(
            [one[:, :width], two[:, :width], one[:, width:], two[:, width:]], axis=1
        )
        both = dot(w1_ref[:, 0:224], stack)
        outer = both[:, 2 * width :]
        first_output(i, 16, both[:, :width], outer[:, :LANES])
        first_output(j, 16, both[:, width : 2 * width], outer[:, LANES:])

    def layer_two(i):
        start = i * 16
        windows = []
        for g in range(2):
            first = start + g * ROWS_OUT
            windows.append(hidden[first : first + ROWS_OUT + 2, :, :].reshape(480, width))
        stack = jnp.concatenate(
            [jnp.concatenate(windows, axis=1), jnp.ones((16, 2 * width), BF16)], axis=0
        )
        deep = jnp.maximum(dot(w2_ref[:, 0:496], stack), 0.0)
        total = hw_ref[0] * deep[0:ROWS_OUT]
        for o in range(1, CH):
            total = total + hw_ref[o] * deep[o * ROWS_OUT : (o + 1) * ROWS_OUT]
        rows = [total[:, :width], total[:, width:]]
        total = jnp.concatenate(rows, axis=0)
        own[start : start + 16, :] = (x_ref[start : start + 16, :].astype(F32) + total).astype(BF16)

    bands = height // PATCH
    bounds = chunk_bounds(height)
    sends = []
    for n in range(len(bounds) - 1):
        rows = pl.ds(bounds[n], bounds[n + 1] - bounds[n])
        if bounds[n + 1] <= height - PATCH:
            target = following.at[rows, :]
        else:
            target = tail_hbm.at[pl.ds(bounds[n] - height + PATCH, bounds[n + 1] - bounds[n]), :]
        sends.append(
            pltpu.make_async_remote_copy(
                src_ref=own.at[rows, :],
                dst_ref=target,
                send_sem=next_send.at[n],
                recv_sem=next_recv.at[n],
                device_id=device(-1, 0, 0),
                device_id_type=MESH,
            )
        )

    early = height - PATCH
    outs = [
        pltpu.make_async_copy(product_ref, product_hbm, out_sem.at[0]),
        pltpu.make_async_copy(spec_ref.at[:, pl.ds(early, PATCH), :], spec_hbm, out_sem.at[1]),
    ]
    table = table_ref[...].astype(BF16)

    layer_one_pair(1, 2)
    layer_one_pair(3, 4)
    receive((0, 1, 4, 5, 6, 7))
    place_edges()
    layer_one_pair(0, blocks_16 - 1)
    for i in range(blocks_16):
        if i % 2 == 0 and i + 6 < blocks_16 - 1:
            layer_one_pair(i + 5, i + 6)
        elif i + 6 == blocks_16 - 1:
            layer_one(blocks_16, 2)
        layer_two(i)
        if (i + 1) * 16 in bounds:
            sends[bounds.index((i + 1) * 16) - 1].start()
        if (i + 1) * 16 % PATCH == 0:
            band = i * 16 // PATCH
            rows = slice(band * PATCH, (band + 1) * PATCH)
            spec_ref[0, rows, :], spec_ref[1, rows, :] = spectrum(own[rows, :], table)

    outs[1].start()
    for n in range(len(sends)):
        if bounds[n + 1] <= early:
            sends[n].wait_recv()
    for band in range(bands - 1):
        rows = slice(band * PATCH, (band + 1) * PATCH)
        other_real, other_imag = spectrum(following[rows, :], table)
        real, imag = spec_ref[0, rows, :], spec_ref[1, rows, :]
        product_ref[0, rows, :] = real * other_real + imag * other_imag
        product_ref[1, rows, :] = imag * other_real - real * other_imag
    outs[0].start()

    for n, (dy, dx) in enumerate(STEPS):

        @pl.when(present(dy, dx))
        def _():
            copies[n].wait_send()

    for n in range(len(sends)):
        sends[n].wait_send()
        if bounds[n + 1] > early:
            sends[n].wait_recv()
    for out in outs:
        out.wait()


def cross_body(
    n_gz,
    product_hbm, spec_hbm, tail_hbm, table_hbm,
    out_hbm,
    spec, tail, table_ref, out_ref, sems, out_sems,
):
    early = out_ref.shape[1] - PATCH
    not_last = lax.axis_index("gz") < n_gz - 1
    outs = [
        pltpu.make_async_copy(
            out_ref.at[:, pl.ds(start, size), :], out_hbm.at[0, :, pl.ds(start, size), :], out_sems.at[n]
        )
        for n, (start, size) in enumerate([(0, early), (early, PATCH)])
    ]

    @pl.when(not_last)
    def _():
        targets = [table_ref, tail, spec, out_ref.at[:, pl.ds(0, early), :]]
        sources = [table_hbm, tail_hbm, spec_hbm, product_hbm]
        loads = [
            pltpu.make_async_copy(source, target, sems.at[n])
            for n, (source, target) in enumerate(zip(sources, targets))
        ]
        for load in loads:
            load.start()
        loads[0].wait()
        table = table_ref[...].astype(BF16)
        loads[1].wait()
        other_real, other_imag = spectrum(tail[...], table)
        loads[2].wait()
        real, imag = spec[0], spec[1]
        out_ref[0, early:, :] = real * other_real + imag * other_imag
        out_ref[1, early:, :] = imag * other_real - real * other_imag
        outs[1].start()
        loads[3].wait()
        outs[0].start()

    @pl.when(jnp.logical_not(not_last))
    def _():
        out_ref[...] = jnp.zeros(out_ref.shape, F32)
        for out in outs:
            out.start()

    for out in outs:
        out.wait()


def on_device(sizes, section, first_kernel, first_bias, second_kernel, second_bias, head_weight):
    height, width = section.shape[1:]
    chunks = len(chunk_bounds(height)) - 1
    hbm = pl.BlockSpec(memory_space=pltpu.HBM)
    table = jnp.asarray(dft_table())
    early = height - PATCH
    product, spec, tail = pl.pallas_call(
        functools.partial(body, sizes),
        out_shape=[
            jax.ShapeDtypeStruct((2, early, width), F32),
            jax.ShapeDtypeStruct((2, PATCH, width), F32),
            jax.ShapeDtypeStruct((PATCH, width), BF16),
        ],
        in_specs=[hbm] * 7,
        out_specs=[hbm] * 3,
        scratch_shapes=[
            pltpu.VMEM((height, width), BF16),
            pltpu.VMEM(first_kernel.shape, F32),
            pltpu.VMEM(second_kernel.shape, BF16),
            pltpu.VMEM((PATCH, 2 * PATCH), F32),
            pltpu.SMEM((CH,), F32),
            pltpu.SMEM((CH,), F32),
            pltpu.SMEM((CH,), F32),
            pltpu.VMEM((height + 2 * EDGE, width + 2 * LANES), BF16),
            pltpu.VMEM((3, height + 2 * EDGE, width + LANES), BF16),
            pltpu.VMEM((height + 16, 3 * CH, width), BF16),
            pltpu.VMEM((height, width), BF16),
            pltpu.VMEM((early, width), BF16),
            pltpu.VMEM((16 * CH, 256), BF16),
            pltpu.VMEM((ROWS_OUT * CH, 512), BF16),
            pltpu.SemaphoreType.DMA((8,)),
            pltpu.SemaphoreType.DMA((8,)),
            pltpu.SemaphoreType.DMA((chunks,)),
            pltpu.SemaphoreType.DMA((chunks,)),
            pltpu.SemaphoreType.DMA((7,)),
            pltpu.VMEM((2, height, width), F32),
            pltpu.VMEM((2, early, width), F32),
            pltpu.SemaphoreType.DMA((2,)),
        ],
        compiler_params=pltpu.CompilerParams(
            collective_id=0, has_side_effects=True, vmem_limit_bytes=64 * 1024 * 1024
        ),
        name="restore_spectra",
    )(section[0], first_kernel, second_kernel, table, first_bias, second_bias, head_weight)
    return pl.pallas_call(
        functools.partial(cross_body, sizes[0]),
        out_shape=jax.ShapeDtypeStruct((1, 2, height, width), F32),
        in_specs=[hbm] * 4,
        out_specs=hbm,
        scratch_shapes=[
            pltpu.VMEM((2, PATCH, width), F32),
            pltpu.VMEM((PATCH, width), BF16),
            pltpu.VMEM((PATCH, 2 * PATCH), F32),
            pltpu.VMEM((2, height, width), F32),
            pltpu.SemaphoreType.DMA((4,)),
            pltpu.SemaphoreType.DMA((2,)),
        ],
        compiler_params=pltpu.CompilerParams(vmem_limit_bytes=64 * 1024 * 1024),
        name="cross_spectra",
    )(product, spec, tail, table)


def solution(mesh):
    sizes = tuple(mesh.shape[name] for name in ("gz", "gy", "gx"))
    placed = (P("gz", "gy", "gx"), P(), P(), P(), P(), P())
    return jax.shard_map(
        functools.partial(on_device, sizes),
        mesh=mesh,
        in_specs=placed,
        out_specs=P("gz", None, "gy", "gx"),
        check_vma=False,
    )
```

```python
import functools
import math

import jax
import jax.numpy as jnp
import numpy as np
from jax import lax
from jax.experimental import pallas as pl
from jax.experimental.pallas import tpu as pltpu
from jax.sharding import PartitionSpec as P

PATCH = 128
CH = 16
EDGE = 16
LANES = 128
ROWS_OUT = 8
F32 = jnp.float32
BF16 = jnp.bfloat16
MESH = pl.DeviceIdType.MESH
SHIFT = jnp.bfloat16
STEPS = [(-1, 0), (1, 0), (0, -1), (0, 1), (-1, -1), (-1, 1), (1, -1), (1, 1)]


def dft_table():
    positions = np.arange(PATCH)
    phase = (positions[:, None] * positions[None, :]) % PATCH
    angles = phase * (2.0 * math.pi / PATCH)
    both = np.concatenate([np.cos(angles), np.sin(angles)], axis=1) / math.sqrt(PATCH)
    return both.astype(np.float32)


def iota(shape, dim):
    return lax.broadcasted_iota(jnp.int32, shape, dim)


def dot(a, b):
    return jnp.dot(a, b, preferred_element_type=F32)


def pieces(value, count):
    out = []
    for _ in range(count):
        part = value.astype(BF16)
        out.append(part)
        value = value - part.astype(F32)
    return out


def column_of(ref):
    ids = iota((CH, 1), 0)
    column = jnp.zeros((CH, 1), F32)
    for c in range(CH):
        column = jnp.where(ids == c, ref[c], column)
    return column


def one_hot(hit):
    return jnp.where(hit, 1.0, 0.0).astype(BF16)


def with_bias(values, ref, lanes, first):
    for n, part in enumerate(pieces(column_of(ref), 3)):
        values = jnp.where(lanes == first + n, part.astype(F32), values)
    return values


def first_weights(kernel_ref, bias_ref, ready):
    rows, depth = 16 * CH, 256
    k = iota((9, depth), 1)
    tap = iota((9, depth), 0)
    col_off = (k & 127) >> 5
    lanes = iota((CH, depth), 1)
    m = iota((rows, depth), 0)
    kk = iota((rows, depth), 1)
    spread = one_hot((iota((rows, CH), 0) & (CH - 1)) == iota((rows, CH), 1))
    fixed = (kk & 127) >= 96
    offset = (kk & 31) - 14 - (m >> 4)
    hits = [(tap == 3 * a + col_off) & (col_off < 3) for a in range(3)]
    places = [(one_hot(hit & (k < 128)), one_hot(hit & (k >= 128))) for hit in hits]
    ready()
    high, low = pieces(kernel_ref[...], 2)
    weights = jnp.zeros((rows, depth), F32)
    for a in range(3):
        placed = dot(high, places[a][0]) + dot(low, places[a][1])
        placed = with_bias(placed, bias_ref, lanes, 96)
        weights = jnp.where(fixed | (offset == a), dot(spread, placed.astype(BF16)), weights)
    return weights.astype(BF16)


def second_weights(kernel_ref, bias_ref, order):
    rows, depth = ROWS_OUT * CH, 512
    flat = kernel_ref[...].reshape(9 * CH, CH)
    tiled = dot(flat, one_hot((iota((CH, depth), 1) & (CH - 1)) == iota((CH, depth), 0)))
    tap = iota((CH, depth), 1) >> 4
    base = jnp.zeros((CH, depth), F32)
    for t in range(9):
        base = jnp.where(tap == t, tiled[t * CH : (t + 1) * CH], base)
    bias = with_bias(jnp.zeros((CH, depth), F32), bias_ref, iota((CH, depth), 1), 480)
    shifted = [base + bias]
    for r in range(1, ROWS_OUT):
        shifted.append(pltpu.roll(base, 3 * CH * r, 1) + bias)
    by_row = jnp.concatenate(shifted, axis=0).astype(BF16)
    return dot(order, by_row).astype(BF16)


def spectrum(image, table):
    cosine, sine = table[:, :PATCH], table[:, PATCH:]
    patches = image.shape[1] // PATCH
    stacked = jnp.concatenate([image[:, n * PATCH : (n + 1) * PATCH] for n in range(patches)], axis=0)
    rows = dot(stacked, table).astype(BF16)
    parts = [rows[n * PATCH : (n + 1) * PATCH] for n in range(patches)]
    lower = jnp.concatenate(
        [
            jnp.concatenate([p[:, :PATCH] for p in parts], axis=1),
            jnp.concatenate([p[:, PATCH:] for p in parts], axis=1),
        ],
        axis=0,
    )
    full = jnp.concatenate(
        [jnp.concatenate([cosine, -sine], axis=1), jnp.concatenate([-sine, -cosine], axis=1)], axis=0
    )
    both = dot(full, lower)
    return both[:PATCH], both[PATCH:]


def chunk_bounds(height):
    return list(range(0, height - 31, 32)) + [height - 16, height]


def body(
    sizes,
    x_hbm, k1_hbm, k2_hbm, table_hbm, b1_hbm, b2_hbm, hw_hbm,
    product_hbm, spec_hbm, tail_hbm,
    x_ref, k1_ref, k2_ref, table_ref, b1_ref, b2_ref, hw_ref,
    halo, shifted, hidden, own, following, w1_ref, w2_ref,
    halo_send, halo_recv, next_send, next_recv, local_sem, spec_ref, product_ref, out_sem,
):
    n_gz, n_gy, n_gx = sizes
    height, width = x_ref.shape
    wide = width + LANES
    near = [k1_ref, b1_ref, k2_ref, b2_ref, x_ref, hw_ref, table_ref]
    far = [k1_hbm, b1_hbm, k2_hbm, b2_hbm, x_hbm, hw_hbm, table_hbm]
    loads = [
        pltpu.make_async_copy(source, target, local_sem.at[n])
        for n, (source, target) in enumerate(zip(far, near))
    ]
    for load in loads:
        load.start()
    gz, gy, gx = lax.axis_index("gz"), lax.axis_index("gy"), lax.axis_index("gx")

    def present(dy, dx):
        y, x = gy + dy, gx + dx
        return (y >= 0) & (y < n_gy) & (x >= 0) & (x < n_gx)

    def device(dz, dy, dx):
        return (
            lax.rem(gz + dz + n_gz, n_gz),
            lax.rem(gy + dy + n_gy, n_gy),
            lax.rem(gx + dx + n_gx, n_gx),
        )

    barrier = pltpu.get_barrier_semaphore()
    count = jnp.int32(2)
    for dy, dx in STEPS:
        count = count + present(dy, dx).astype(jnp.int32)

        @pl.when(present(dy, dx))
        def _():
            pl.semaphore_signal(barrier, inc=1, device_id=device(0, dy, dx), device_id_type=MESH)

    for dz in (-1, 1):
        pl.semaphore_signal(barrier, inc=1, device_id=device(dz, 0, 0), device_id_type=MESH)

    pl.semaphore_wait(barrier, count)

    row_src = {-1: (0, EDGE), 1: (height - EDGE, EDGE), 0: (0, height)}
    col_src = {-1: (0, LANES), 1: (width - LANES, LANES), 0: (0, width)}
    row_dst = {-1: EDGE + height, 1: 0, 0: EDGE}
    col_dst = {-1: width, 1: width + LANES, 0: 0}
    copies = []
    for n, (dy, dx) in enumerate(STEPS):
        (r0, rn), (c0, cn) = row_src[dy], col_src[dx]
        copies.append(
            pltpu.make_async_remote_copy(
                src_ref=x_hbm.at[pl.ds(r0, rn), pl.ds(c0, cn)],
                dst_ref=halo.at[pl.ds(row_dst[dy], rn), pl.ds(col_dst[dx], cn)],
                send_sem=halo_send.at[n],
                recv_sem=halo_recv.at[n],
                device_id=device(0, dy, dx),
                device_id_type=MESH,
            )
        )
    for n, (dy, dx) in enumerate(STEPS):

        @pl.when(present(dy, dx))
        def _():
            copies[n].start()

        @pl.when(jnp.logical_not(present(-dy, -dx)))
        def _():
            rn, cn = row_src[dy][1], col_src[dx][1]
            halo[pl.ds(row_dst[dy], rn), pl.ds(col_dst[dx], cn)] = jnp.zeros((rn, cn), BF16)

    pair = (ROWS_OUT * CH, ROWS_OUT * CH)
    m, n = iota(pair, 0), iota(pair, 1)
    order = one_hot(n == (m & (ROWS_OUT - 1)) * CH + (m >> 3))

    def ready():
        for load in loads[:4]:
            load.wait()

    w1_ref[...] = first_weights(k1_ref, b1_ref, ready)
    w2_ref[...] = second_weights(k2_ref, b2_ref, order)
    for load in loads[4:]:
        load.wait()

    def receive(chosen):
        for n in chosen:
            dy, dx = STEPS[n]

            @pl.when(present(-dy, -dx))
            def _():
                copies[n].wait_recv()

    def shift(blocks, step, before, after):
        lane = iota(blocks[0].shape, 1)
        rolled = [pltpu.roll(block, step % LANES, 1) for block in blocks]
        if step > 0:
            fill = [before] + rolled[:-1]
            return [jnp.where(lane == 0, f, r) for f, r in zip(fill, rolled)]
        fill = rolled[1:] + [after]
        return [jnp.where(lane == LANES - 1, f, r) for f, r in zip(fill, rolled)]

    def place(row, size, centre):
        lane = iota((size, LANES), 1)
        right = halo[row : row + size, width : width + LANES]
        left = halo[row : row + size, width + LANES : width + 2 * LANES]
        blocks = [centre[:, n : n + LANES] for n in range(0, width, LANES)]
        left_1, right_1 = pltpu.roll(left, 1, 1), pltpu.roll(right, LANES - 1, 1)
        taps = [
            shift(blocks, 1, left_1, None)
            + [jnp.where(lane == LANES - 1, blocks[-1], pltpu.roll(left, 2, 1))],
            blocks + [jnp.where(lane == LANES - 1, right_1, left_1)],
            shift(blocks, -1, None, right_1)
            + [jnp.where(lane == LANES - 1, pltpu.roll(right, LANES - 2, 1), blocks[0])],
        ]
        for b in range(3):
            shifted[b, row : row + size, :] = jnp.concatenate(taps[b], axis=1)

    def place_edges():
        place(0, EDGE, halo[0:EDGE, 0:width])
        place(EDGE + height, EDGE, halo[EDGE + height : 2 * EDGE + height, 0:width])

    receive((2, 3))
    for row in range(0, height, 64):
        place(EDGE + row, 64, x_ref[row : row + 64, :])

    lane = iota((1, LANES), 1)
    keep = ((lane == 0) & (gx > 0)) | ((lane == LANES - 1) & (gx < n_gx - 1))
    keep = jnp.where(keep, 1.0, 0.0)
    above = jnp.where(gy > 0, 1.0, 0.0)
    below = jnp.where(gy < n_gy - 1, 1.0, 0.0)
    blocks_16 = height // 16

    def first_input(i):
        start = i * 16
        taps = [shifted[b, start : start + 32, :] for b in range(3)]
        return jnp.concatenate(taps + [jnp.ones((32, wide), BF16)] + taps, axis=0)

    def first_output(i, rows, value, outer):
        start = i * 16
        value, outer = jnp.maximum(value, 0.0), jnp.maximum(outer, 0.0) * keep
        if i == 0:
            value = jnp.concatenate([value[:CH] * above, value[CH:]], axis=0)
            outer = jnp.concatenate([outer[:CH] * above, outer[CH:]], axis=0)
        if i == blocks_16:
            value = jnp.concatenate([value[:CH], value[CH : 2 * CH] * below], axis=0)
            outer = jnp.concatenate([outer[:CH], outer[CH : 2 * CH] * below], axis=0)
        outer = outer.astype(SHIFT)
        blocks = [value[:, n : n + LANES].astype(SHIFT) for n in range(0, width, LANES)]
        for b, part in enumerate([shift(blocks, 1, outer, None), blocks, shift(blocks, -1, None, outer)]):
            hidden[start : start + rows, b * CH : (b + 1) * CH, :] = (
                jnp.concatenate(part, axis=1).reshape(rows, CH, width)
            )

    def layer_one(i, rows):
        value = dot(w1_ref[0 : rows * CH, 0:224], first_input(i))
        first_output(i, rows, value[:, :width], value[:, width:])

    def layer_one_pair(i, j):
        one, two = first_input(i), first_input(j)
        weights = w1_ref[:, 0:224]
        outer = dot(weights, jnp.concatenate([one[:, width:], two[:, width:]], axis=1))
        first_output(i, 16, dot(weights, one[:, :width]), outer[:, :LANES])
        first_output(j, 16, dot(weights, two[:, :width]), outer[:, LANES:])

    def layer_two(i):
        start = i * 16
        rows = []
        for g in range(2):
            first = start + g * ROWS_OUT
            window = hidden[first : first + ROWS_OUT + 2, :, :].reshape(480, width)
            stack = jnp.concatenate([window, jnp.ones((16, width), BF16)], axis=0)
            deep = jnp.maximum(dot(w2_ref[:, 0:496], stack), 0.0)
            total = hw_ref[0] * deep[0:ROWS_OUT]
            for o in range(1, CH):
                total = total + hw_ref[o] * deep[o * ROWS_OUT : (o + 1) * ROWS_OUT]
            rows.append(total)
        total = jnp.concatenate(rows, axis=0)
        own[start : start + 16, :] = (x_ref[start : start + 16, :].astype(F32) + total).astype(BF16)

    bands = height // PATCH
    bounds = chunk_bounds(height)
    sends = []
    for n in range(len(bounds) - 1):
        rows = pl.ds(bounds[n], bounds[n + 1] - bounds[n])
        if bounds[n + 1] <= height - PATCH:
            target = following.at[rows, :]
        else:
            target = tail_hbm.at[pl.ds(bounds[n] - height + PATCH, bounds[n + 1] - bounds[n]), :]
        sends.append(
            pltpu.make_async_remote_copy(
                src_ref=own.at[rows, :],
                dst_ref=target,
                send_sem=next_send.at[n],
                recv_sem=next_recv.at[n],
                device_id=device(-1, 0, 0),
                device_id_type=MESH,
            )
        )

    early = height - PATCH
    outs = [
        pltpu.make_async_copy(product_ref, product_hbm, out_sem.at[0]),
        pltpu.make_async_copy(spec_ref.at[:, pl.ds(early, PATCH), :], spec_hbm, out_sem.at[1]),
    ]
    table = table_ref[...].astype(BF16)

    layer_one_pair(1, 2)
    layer_one_pair(3, 4)
    receive((0, 1, 4, 5, 6, 7))
    place_edges()
    layer_one_pair(0, blocks_16 - 1)
    for i in range(blocks_16):
        if i % 2 == 0 and i + 6 < blocks_16 - 1:
            layer_one_pair(i + 5, i + 6)
        elif i + 6 == blocks_16 - 1:
            layer_one(blocks_16, 2)
        layer_two(i)
        if (i + 1) * 16 in bounds:
            sends[bounds.index((i + 1) * 16) - 1].start()
        if (i + 1) * 16 % PATCH == 0:
            band = i * 16 // PATCH
            rows = slice(band * PATCH, (band + 1) * PATCH)
            spec_ref[0, rows, :], spec_ref[1, rows, :] = spectrum(own[rows, :], table)

    outs[1].start()
    for n in range(len(sends)):
        if bounds[n + 1] <= early:
            sends[n].wait_recv()
    for band in range(bands - 1):
        rows = slice(band * PATCH, (band + 1) * PATCH)
        other_real, other_imag = spectrum(following[rows, :], table)
        real, imag = spec_ref[0, rows, :], spec_ref[1, rows, :]
        product_ref[0, rows, :] = real * other_real + imag * other_imag
        product_ref[1, rows, :] = imag * other_real - real * other_imag
    outs[0].start()

    for n, (dy, dx) in enumerate(STEPS):

        @pl.when(present(dy, dx))
        def _():
            copies[n].wait_send()

    for n in range(len(sends)):
        sends[n].wait_send()
        if bounds[n + 1] > early:
            sends[n].wait_recv()
    for out in outs:
        out.wait()


def cross_body(
    n_gz,
    product_hbm, spec_hbm, tail_hbm, table_hbm,
    out_hbm,
    spec, tail, table_ref, out_ref, sems, out_sems,
):
    early = out_ref.shape[1] - PATCH
    not_last = lax.axis_index("gz") < n_gz - 1
    outs = [
        pltpu.make_async_copy(
            out_ref.at[plane, pl.ds(start, size), :],
            out_hbm.at[0, plane, pl.ds(start, size), :],
            out_sems.at[n],
        )
        for n, (plane, start, size) in enumerate(
            [(0, 0, early), (1, 0, early), (0, early, PATCH), (1, early, PATCH)]
        )
    ]

    @pl.when(not_last)
    def _():
        targets = [table_ref, tail, spec, out_ref.at[:, pl.ds(0, early), :]]
        sources = [table_hbm, tail_hbm, spec_hbm, product_hbm]
        loads = [
            pltpu.make_async_copy(source, target, sems.at[n])
            for n, (source, target) in enumerate(zip(sources, targets))
        ]
        for load in loads:
            load.start()
        loads[0].wait()
        table = table_ref[...].astype(BF16)
        loads[1].wait()
        other_real, other_imag = spectrum(tail[...], table)
        loads[2].wait()
        real, imag = spec[0], spec[1]
        loads[3].wait()
        outs[0].start()
        outs[1].start()
        out_ref[0, early:, :] = real * other_real + imag * other_imag
        outs[2].start()
        out_ref[1, early:, :] = imag * other_real - real * other_imag
        outs[3].start()

    @pl.when(jnp.logical_not(not_last))
    def _():
        out_ref[...] = jnp.zeros(out_ref.shape, F32)
        for out in outs:
            out.start()

    for out in outs:
        out.wait()


def on_device(sizes, section, first_kernel, first_bias, second_kernel, second_bias, head_weight):
    height, width = section.shape[1:]
    chunks = len(chunk_bounds(height)) - 1
    hbm = pl.BlockSpec(memory_space=pltpu.HBM)
    table = jnp.asarray(dft_table())
    early = height - PATCH
    product, spec, tail = pl.pallas_call(
        functools.partial(body, sizes),
        out_shape=[
            jax.ShapeDtypeStruct((2, early, width), F32),
            jax.ShapeDtypeStruct((2, PATCH, width), F32),
            jax.ShapeDtypeStruct((PATCH, width), BF16),
        ],
        in_specs=[hbm] * 7,
        out_specs=[hbm] * 3,
        scratch_shapes=[
            pltpu.VMEM((height, width), BF16),
            pltpu.VMEM(first_kernel.shape, F32),
            pltpu.VMEM(second_kernel.shape, BF16),
            pltpu.VMEM((PATCH, 2 * PATCH), F32),
            pltpu.SMEM((CH,), F32),
            pltpu.SMEM((CH,), F32),
            pltpu.SMEM((CH,), F32),
            pltpu.VMEM((height + 2 * EDGE, width + 2 * LANES), BF16),
            pltpu.VMEM((3, height + 2 * EDGE, width + LANES), BF16),
            pltpu.VMEM((height + 16, 3 * CH, width), BF16),
            pltpu.VMEM((height, width), BF16),
            pltpu.VMEM((early, width), BF16),
            pltpu.VMEM((16 * CH, 256), BF16),
            pltpu.VMEM((ROWS_OUT * CH, 512), BF16),
            pltpu.SemaphoreType.DMA((8,)),
            pltpu.SemaphoreType.DMA((8,)),
            pltpu.SemaphoreType.DMA((chunks,)),
            pltpu.SemaphoreType.DMA((chunks,)),
            pltpu.SemaphoreType.DMA((7,)),
            pltpu.VMEM((2, height, width), F32),
            pltpu.VMEM((2, early, width), F32),
            pltpu.SemaphoreType.DMA((2,)),
        ],
        compiler_params=pltpu.CompilerParams(
            collective_id=0, has_side_effects=True, vmem_limit_bytes=64 * 1024 * 1024
        ),
        name="restore_spectra",
    )(section[0], first_kernel, second_kernel, table, first_bias, second_bias, head_weight)
    return pl.pallas_call(
        functools.partial(cross_body, sizes[0]),
        out_shape=jax.ShapeDtypeStruct((1, 2, height, width), F32),
        in_specs=[hbm] * 4,
        out_specs=hbm,
        scratch_shapes=[
            pltpu.VMEM((2, PATCH, width), F32),
            pltpu.VMEM((PATCH, width), BF16),
            pltpu.VMEM((PATCH, 2 * PATCH), F32),
            pltpu.VMEM((2, height, width), F32),
            pltpu.SemaphoreType.DMA((4,)),
            pltpu.SemaphoreType.DMA((4,)),
        ],
        compiler_params=pltpu.CompilerParams(vmem_limit_bytes=64 * 1024 * 1024),
        name="cross_spectra",
    )(product, spec, tail, table)


def solution(mesh):
    sizes = tuple(mesh.shape[name] for name in ("gz", "gy", "gx"))
    placed = (P("gz", "gy", "gx"), P(), P(), P(), P(), P())
    return jax.shard_map(
        functools.partial(on_device, sizes),
        mesh=mesh,
        in_specs=placed,
        out_specs=P("gz", None, "gy", "gx"),
        check_vma=False,
    )
```
